32 devices in a mesh: groups: 2 (over y), cls: 8 (over z, x), dom: 2 (over core).
Axes of the slice: x: 2, y: 2, z: 4, core: 2. Of those that a mesh axis runs over, the one named last changes fastest.
Arguments:
- particles: bfloat16 [128, 18432], P(('groups', 'cls', 'dom')), parts along dimension 0, may hold values from -80 to 80
- references: bfloat16 [128, 18432], P(('groups', 'cls')), parts along dimension 0, may hold values from -6 to 6
- class_lists: int32 [128, 32], P(('groups', 'cls', 'dom')), parts along dimension 0, may hold values from 0 to 63, as said below
- offsets: int32 [128, 3, 2], P(('groups', 'cls', 'dom')), parts along dimension 0, may hold values from -8 to 8
- inv_noise: float32 [64], replicated, may hold values from 0.004 to 0.03
Outputs:
- class_sums: float32 [128, 18432], P(('groups', 'cls'), 'dom'), parts along dimension 0
- log_evidence: float32 [128], P(('groups', 'cls', 'dom')), parts along dimension 0
The draws below stay inside these ranges and needn't reach their ends.
There are 2 independent parts, one for each index of `groups`. The reference program is written for one: setup_inputs(seed, part) draws one part's arguments, and reference() takes and returns one part's arrays. A program takes and returns all parts, laid end to end along the dimension named above; an argument that names none is the same for every part. Nothing has to cross between parts.
Inputs may be any that keep to these rules, and one draw needn't show every extreme that they name: `class_lists`: each particle names 32 different classes, the j-th of them in [j * 2, (j + 1) * 2). Among the particles on the devices of one dom index, at most 32 name any one class, and some class is named by exactly 32 of them.
All inputs are finite; a program needn't handle non-finite values.
Results may differ from the reference program's by a relative error of at most 0.0083.
Values may be sent and summed in bfloat16 or wider, within the bound.
No kernel may reach another device: no remote copies, remote signals or barrier semaphores. Data moves between devices by JAX's collectives and lax.ppermute only.
A program may use at most 192 MiB of HBM per device.

```python
import math
import jax
import jax.numpy as jnp
from jax import lax

CYCLES = 64
ROT = 72
CLS_DEV = 8
CLASS_LIST_SIZE = 32
TRANS = 3
BOX = 256
OFFMAX = 8
P_DEV = 4
IMAGE_REALS = 18432
LINES = 256
CLASSES = 64
PARTICLES = 64
N_CLS = 8
N_DOM = 2


def class_table(base):
    half_rows = N_CLS * P_DEV
    band_width = CLASSES // CLASS_LIST_SIZE
    mean_load = P_DEV * CLASS_LIST_SIZE // CLS_DEV
    capacity = 2 * mean_load
    source = jax.random.fold_in(base, 101)

    def one_band(half_index, band_index):
        band_key = jax.random.fold_in(jax.random.fold_in(source, half_index), band_index)
        order = jax.random.permutation(jax.random.fold_in(band_key, 1), half_rows)
        placed = jnp.argsort(order, stable=True).astype(jnp.int32)
        hottest = jax.random.randint(jax.random.fold_in(band_key, 2), (), 0, band_width)
        loaded = jax.random.randint(jax.random.fold_in(band_key, 3), (), mean_load, capacity + 1)
        loaded = jnp.where(band_index == 0, capacity, loaded)
        ranked = (placed - loaded) * (band_width - 1) // jnp.maximum(half_rows - loaded, 1)
        others = ranked + (ranked >= hottest).astype(jnp.int32)
        picked = jnp.where(placed < loaded, hottest, others)
        return band_index * band_width + picked

    def one_half(half_index):
        bands = jnp.arange(CLASS_LIST_SIZE, dtype=jnp.int32)
        return jax.vmap(partial_band(one_band, half_index))(bands)
    halves = jnp.arange(N_DOM, dtype=jnp.int32)
    table = jax.vmap(one_half)(halves)
    table = jnp.transpose(table, (0, 2, 1)).reshape(N_DOM, N_CLS, P_DEV, CLASS_LIST_SIZE)
    table = jnp.transpose(table, (1, 0, 2, 3)).reshape(PARTICLES, CLASS_LIST_SIZE)
    return table.astype(jnp.int32)


def partial_band(function, half_index):

    def inner(band_index):
        return function(half_index, band_index)
    return inner


def offset_table(base):
    return jax.random.randint(jax.random.fold_in(base, 202), (PARTICLES, TRANS, 2), -OFFMAX, OFFMAX + 1).astype(jnp.int32)


def reference_table(base):
    return jax.random.truncated_normal(jax.random.fold_in(base, 303), -6.0, 6.0, (CLASSES, IMAGE_REALS), jnp.float32)


def draw_class_lists(key, part):
    return class_table(key)


def draw_offsets(key, part):
    return offset_table(key)


def draw_references(key, part):
    return reference_table(key).astype(jnp.bfloat16)


def draw_particles(key, part):
    own = jax.random.fold_in(key, 4)
    return jax.random.truncated_normal(own, -6.0, 6.0, (PARTICLES, IMAGE_REALS), jnp.float32).astype(jnp.bfloat16)


def setup_inputs(seed: int = 0, part: int = 0) -> dict:
    key_list = jax.random.split(jax.random.key(seed), 6)
    part_keys = jax.random.split(jax.random.fold_in(key_list[5], part), 6)
    return {
        "particles": draw_particles(jax.random.fold_in(jax.random.fold_in(key_list[5], part), 71), part),
        "references": draw_references(jax.random.fold_in(jax.random.fold_in(key_list[5], part), 71), part),
        "class_lists": draw_class_lists(jax.random.fold_in(jax.random.fold_in(key_list[5], part), 71), part),
        "offsets": draw_offsets(jax.random.fold_in(jax.random.fold_in(key_list[5], part), 71), part),
        "inv_noise": jnp.clip(jnp.exp(jax.random.uniform(key_list[4], (CYCLES,), jnp.float32, math.log(0.004), math.log(0.03))), 0.004, 0.03),
    }


def angle_tables(cycles, turns):
    value_index = jnp.arange(cycles * 2 * turns, dtype=jnp.int32)
    cycle_index = value_index // (2 * turns)
    angle_index = value_index % (2 * turns)
    parity = angle_index // turns
    turn_index = angle_index % turns
    radius = (cycle_index + 1).astype(jnp.float32)
    angle_value = (2 * turn_index + parity).astype(jnp.float32) * jnp.float32(math.pi / turns)
    return radius * jnp.cos(angle_value), radius * jnp.sin(angle_value)


def shift_rows(rows, moves, freq_x, freq_y):
    step_x = moves[..., 0:1].astype(jnp.float32)
    step_y = moves[..., 1:2].astype(jnp.float32)
    phase = (freq_x * step_x + freq_y * step_y) * jnp.float32(2.0 * math.pi / BOX)
    half_width = rows.shape[-1] // 2
    real_part = rows[:, None, :half_width].astype(jnp.float32)
    imag_part = rows[:, None, half_width:].astype(jnp.float32)
    cosine = jnp.cos(phase)
    sine = jnp.sin(phase)
    joined = jnp.concatenate([real_part * cosine + imag_part * sine, imag_part * cosine - real_part * sine], axis=-1)
    return joined.astype(jnp.bfloat16)


def cycle_weights(inv_noise, turns):
    return jnp.tile(jnp.repeat(inv_noise.astype(jnp.float32), 2 * turns), 2)


def turn_table(turns, sign):
    first = jnp.arange(turns, dtype=jnp.int32)[:, None]
    second = jnp.arange(turns, dtype=jnp.int32)[None, :]
    return (first + sign * second) % turns


def reference(particles, references, class_lists, offsets, inv_noise):
    freq_x, freq_y = angle_tables(CYCLES, ROT)
    scaled = (references.astype(jnp.float32) * cycle_weights(inv_noise, ROT)).astype(jnp.bfloat16)
    shifted_all = shift_rows(particles, offsets, freq_x, freq_y)
    ahead = turn_table(ROT, 1)

    def one_particle(carry, inputs):
        shifted, picks = inputs
        stacked = shifted.reshape(TRANS, LINES, ROT).astype(jnp.float32)
        rotated_images = jnp.take(stacked, ahead, axis=2)
        selected_classes = scaled[picks].reshape(CLASS_LIST_SIZE, LINES, ROT).astype(jnp.float32)
        class_scores = jnp.einsum("yqsm,zqs->zym", rotated_images, selected_classes)
        top = jnp.max(class_scores, axis=(1, 2))
        expo = jnp.exp(class_scores - top[:, None, None])
        total = jnp.sum(expo, axis=(1, 2))
        posterior_weight = lax.optimization_barrier(expo.astype(jnp.bfloat16)).astype(jnp.float32)
        best = jnp.max(top)
        evidence = jnp.sum(total * jnp.exp(top - best))
        returned_sums = jnp.einsum("owd,wqsd->oqs", posterior_weight, rotated_images).reshape(CLASS_LIST_SIZE, IMAGE_REALS)
        factor = jnp.exp(top - best) / evidence
        carry = carry.at[picks].add(returned_sums * factor[:, None])
        return carry, best + jnp.log(evidence)

    start = jnp.zeros((CLASSES, IMAGE_REALS), jnp.float32)
    sums, log_evidence = lax.scan(one_particle, start, (shifted_all, class_lists))
    return sums, log_evidence
```

```python
import math

import jax
import jax.numpy as jnp
import numpy as np
from jax import lax
from jax.experimental import pallas as pl
from jax.experimental.pallas import tpu as pltpu
from jax.sharding import PartitionSpec as P

ROT = 72
CYCLES = 64
CLASS_LIST_SIZE = 32
BOX = 256
TRANS = 3
PER_DEV = 4
CLS = 8
SLOTS = 8
LANES = 256
HALF = 128
GROUP = 16 * ROT
ROWS = ROT * PER_DEV
REF_ROWS = ROT * CLS
PAIRS = ROT // 2
LOWEST = -1e30
VMEM = 48 * 1024 * 1024

F32 = jnp.float32
BF16 = jnp.bfloat16


def frequency_rows():
    turn = np.arange(ROT)[:, None]
    lane = np.arange(HALF)[None, :]
    line = (lane % 8) * 16 + lane // 8
    radius = line // 2 + 1
    angle = math.pi * (2 * turn + line % 2) / ROT
    fx = radius * np.cos(angle) / BOX
    fy = radius * np.sin(angle) / BOX
    rep = lambda f: np.repeat(f, PER_DEV, axis=0).astype(np.float32)
    return rep(fx), rep(fy)


def half_turn_polynomials():
    t = np.cos(np.pi * (np.arange(400) + 0.5) / 400)
    z = (t + 1) / 8
    v = np.sqrt(z)
    sin_fit = np.polynomial.chebyshev.Chebyshev.fit(z, np.sin(np.pi * v) / v, 4, domain=[0, 0.25])
    cos_fit = np.polynomial.chebyshev.Chebyshev.fit(z, np.cos(np.pi * v), 5, domain=[0, 0.25])
    to_list = lambda f: [float(c) for c in f.convert(kind=np.polynomial.Polynomial).coef]
    return to_list(sin_fit), to_list(cos_fit)


SIN_COEF, COS_COEF = half_turn_polynomials()


def horner(coef, z):
    total = jnp.full_like(z, coef[-1])
    for c in coef[-2::-1]:
        total = total * z + c
    return total


def cos_sin_turns(u):
    v = u - jnp.round(u)
    z = v * v
    s = v * horner(SIN_COEF, z)
    c = horner(COS_COEF, z)
    s2 = s + s
    return 1.0 - s2 * s, s2 * c


def turn_major(x_ref, grid_ref, lines_ref, out_ref, count):
    for g in range(16):
        for tile in range(GROUP // HALF):
            start = g * GROUP + tile * HALF
            grid_ref[tile, pl.ds(g, count, stride=16), :] = x_ref[:, start : start + HALF].astype(F32)
    for h in range(16):
        tile, shift = divmod(ROT * h, HALF)
        if shift + ROT <= HALF:
            part = grid_ref[tile]
            if shift:
                part = pltpu.roll(part, HALF - shift, 1)
        else:
            part = jnp.concatenate([grid_ref[tile], grid_ref[tile + 1]], axis=1)
            part = pltpu.roll(part, LANES - shift, 1)[:, :HALF]
        lines_ref[:, :, h] = part.reshape(count, 2, 8, HALF)
    for p in range(count):
        for half in range(2):
            turns = lines_ref[p, half].reshape(HALF, HALF).T
            out_ref[half, pl.ds(p, ROT, stride=count), :] = turns[:ROT]


def particle_kernel(nbit, x_ref, list_ref, move_ref, out_ref, grid_ref, lines_ref, turns_ref):
    turn_major(x_ref, grid_ref, lines_ref, turns_ref, PER_DEV)
    out_ref[:ROWS] = jnp.concatenate([turns_ref[0], turns_ref[1]], axis=1).astype(BF16)
    lists = list_ref[...]
    lane = lax.broadcasted_iota(jnp.int32, (PER_DEV, LANES), 1)
    parts = []
    for b in range(nbit):
        named = jnp.zeros((PER_DEV, LANES), F32)
        for j in range(CLASS_LIST_SIZE):
            named = jnp.where(lists[:, j : j + 1] == lane + b * LANES, 1.0, named)
        parts += [named, named]
    row = lax.broadcasted_iota(jnp.int32, (8, LANES), 0) % PER_DEV
    lane = lax.broadcasted_iota(jnp.int32, (8, LANES), 1)
    moves = jnp.zeros((8, LANES), F32)
    for p in range(PER_DEV):
        for t in range(TRANS):
            for a in range(2):
                here = (row == p) & (lane == 8 * a + t)
                moves = jnp.where(here, move_ref[p, t, a].astype(F32), moves)
    parts.append(moves)
    if nbit % 2 == 0:
        parts.append(jnp.zeros((8, LANES), F32))
    out_ref[ROWS:] = jnp.concatenate(parts, axis=0).astype(BF16)


def reference_kernel(x_ref, w_ref, out_ref, grid_ref, lines_ref, turns_ref):
    turn_major(x_ref, grid_ref, lines_ref, turns_ref, CLS)
    scaled = (jnp.concatenate([turns_ref[0], turns_ref[1]], axis=1) * w_ref[...]).astype(BF16)
    out_ref[:REF_ROWS] = scaled
    out_ref[REF_ROWS:] = scaled


def xor_lanes(x, bits):
    lane = lax.broadcasted_iota(jnp.int32, x.shape, x.ndim - 1)
    width = x.shape[-1]
    for b in range(3):
        if bits >> b & 1:
            step = 8 << b
            down = pltpu.roll(x, width - step, x.ndim - 1)
            up = pltpu.roll(x, step, x.ndim - 1)
            x = jnp.where((lane // step) % 2 == 0, down, up)
    return x


def score_kernel(nbit, me_ref, *refs):
    blocks = refs[:SLOTS]
    fx_ref, fy_ref, ref_ref, x_ref, e_ref, stat_ref, acc_ref = refs[SLOTS:]
    moves = []
    for s in range(SLOTS):
        m = blocks[s][0, ROWS + 8 * nbit - 8 * (nbit % 2) : ROWS + 8 * nbit + 16 - 8 * (nbit % 2)].astype(F32)
        m = m[8 * (nbit % 2) : 8 * (nbit % 2) + 8]
        m = jnp.concatenate([m, m], axis=0)
        moves.append([
            (jnp.broadcast_to(m[:, t : t + 1], (16, HALF)), jnp.broadcast_to(m[:, 8 + t : 9 + t], (16, HALF)))
            for t in range(TRANS)
        ])
    acc_ref[...] = jnp.zeros_like(acc_ref)

    def step(q, carry):
        rows = pl.ds(pl.multiple_of(q * 16, 16), 16)
        fx = fx_ref[rows, :]
        fy = fy_ref[rows, :]
        tiles = [[None] * SLOTS for _ in range(TRANS)]
        for s in range(SLOTS):
            block = blocks[s][0, rows, :].astype(F32)
            a = block[:, :HALF]
            b = block[:, HALF:]
            for t in range(TRANS):
                dx, dy = moves[s][t]
                c, sn = cos_sin_turns(fx * dx + fy * dy)
                tiles[t][s] = (a * c + b * sn, b * c - a * sn)
        for half in range(2):
            packed = []
            for t in range(TRANS):
                for s in range(0, SLOTS, 2):
                    cols = [
                        jnp.concatenate(
                            [tiles[t][s][r][half * 8 : half * 8 + 8], tiles[t][s + 1][r][half * 8 : half * 8 + 8]],
                            axis=0,
                        )
                        for r in range(2)
                    ]
                    packed.append(jnp.concatenate(cols, axis=1).astype(BF16))
            packed.append(jnp.zeros((64, LANES), BF16))
            images = jnp.concatenate(packed, axis=0)
            x_ref[0, 2 * q + half] = images
            turned = ref_ref[pl.ds(pl.multiple_of((2 * q + half) * 16, 16), REF_ROWS), :]
            acc_ref[...] += lax.dot_general(turned, images, (((1,), (1,)), ((), ())), preferred_element_type=F32)
        return carry

    lax.fori_loop(0, PAIRS // 2, step, 0)

    me = me_ref[0]
    lane = lax.broadcasted_iota(jnp.int32, (CLS, LANES), 1)
    row = lax.broadcasted_iota(jnp.int32, (CLS, LANES), 0)
    named = jnp.zeros((CLS, SLOTS * 16), F32)
    for b in range(nbit):
        pick = (lane + b * LANES == me * CLS + row).astype(F32).astype(BF16)
        first = ROWS + 16 * (b // 2)
        bits = jnp.concatenate([blocks[s][0, first : first + 16] for s in range(SLOTS)], axis=0)
        got = lax.dot_general(pick, bits, (((1,), (1,)), ((), ())), preferred_element_type=F32)
        if b % 2:
            got = pltpu.roll(got, SLOTS * 16 - 8, 1)
        named = named + got
    src = lax.broadcasted_iota(jnp.int32, (SLOTS * 16, LANES), 0)
    dst = lax.broadcasted_iota(jnp.int32, (SLOTS * 16, LANES), 1)
    wanted_row = (dst % 64) // 8 * 16 + dst % PER_DEV
    ok = (src == wanted_row) & (dst < 64 * TRANS) & (dst % 8 < PER_DEV)
    mask = jnp.dot(named.astype(BF16), ok.astype(F32).astype(BF16), preferred_element_type=F32) > 0.5

    def body_max(i, top):
        nxt = jnp.where(i == ROT - 1, 0, i + 1)
        s = acc_ref[pl.ds(pl.multiple_of(i * 8, 8), 8), :]
        o = acc_ref[pl.ds(pl.multiple_of(nxt * 8, 8), 8), :]
        s = jnp.where(mask, s + pltpu.roll(o, LANES - 4, 1), LOWEST)
        e_ref[0, pl.ds(pl.multiple_of(i * 8, 8), 8), :] = s
        return jnp.maximum(top, s)

    top = lax.fori_loop(0, ROT, body_max, jnp.full((CLS, LANES), LOWEST, F32), unroll=8)
    top = jnp.max(top, axis=0, keepdims=True)
    top = jnp.broadcast_to(top, (8, LANES))
    for shift in (64, 128):
        top = jnp.maximum(top, pltpu.roll(top, shift, 1))

    def body_exp(i, total):
        rows = pl.ds(pl.multiple_of(i * 8, 8), 8)
        e = jnp.where(mask, jnp.exp(e_ref[0, rows, :] - top), 0.0)
        e_ref[0, rows, :] = e
        return total + e

    total = lax.fori_loop(0, ROT, body_exp, jnp.zeros((CLS, LANES), F32), unroll=8)
    total = jnp.broadcast_to(jnp.sum(total, axis=0, keepdims=True), (8, LANES))
    for shift in (64, 128):
        total = total + pltpu.roll(total, shift, 1)
    first = lax.broadcasted_iota(jnp.int32, (8, HALF), 0) == 0
    stat_ref[0] = jnp.where(first, top[:, :HALF], total[:, :HALF])


def spread_kernel(holders, me_ref, stat_ref, out_ref):
    blocks = holders // SLOTS
    me = me_ref[0]
    for low in range(SLOTS):
        for n in range(blocks):
            moved = xor_lanes(stat_ref[n], low)
            for high in range(blocks):
                out_ref[me ^ (high * SLOTS + low), n ^ high] = moved


def back_kernel(holders, me_ref, got_ref, stat_ref, e_ref, x_ref, keep_ref, send_ref, log_ref, w_ref, acc_ref):
    n = pl.program_id(0)
    top = got_ref[0, n]
    for d in range(1, holders):
        top = jnp.maximum(top, got_ref[d, n])
    best = jnp.broadcast_to(top[0:1], (8, HALF))
    evidence = jnp.zeros((8, HALF), F32)
    for d in range(holders):
        got = got_ref[d, n]
        one = jnp.broadcast_to(got[0:1], (8, HALF))
        evidence = evidence + jnp.broadcast_to(got[1:2], (8, HALF)) * jnp.exp(one - best)
    own = jnp.broadcast_to(stat_ref[0, 0:1], (8, HALF))
    factor = jnp.exp(own - best) / evidence

    @pl.when(n == 0)
    def _():
        log_ref[...] = best + jnp.log(evidence)
        acc_ref[...] = jnp.zeros_like(acc_ref)

    factor = jnp.concatenate([factor, factor], axis=1)
    lane = lax.broadcasted_iota(jnp.int32, (8, LANES), 1)
    live = (lane % 8 < PER_DEV) & (lane < 64 * TRANS)
    factor = jnp.where(live, factor, 0.0)

    def weights(i):
        return jnp.where(live, e_ref[0, i * 8 : i * 8 + 8, :] * factor, 0.0)

    before = weights(ROT - 1)
    for i in range(0, ROT, 2):
        one = weights(i)
        two = weights(i + 1)
        pair = jnp.concatenate(
            [one + pltpu.roll(before, 4, 1), two + pltpu.roll(one, 4, 1)], axis=0
        ).astype(BF16)
        w_ref[i * 8 : i * 8 + 16, :] = pair
        w_ref[REF_ROWS + i * 8 : REF_ROWS + i * 8 + 16, :] = pair
        before = two

    def step(q, carry):
        total = acc_ref[...]
        for r in range(4):
            j = 4 * q + r
            turned = w_ref[pl.ds(pl.multiple_of((PAIRS - j) * 16, 16), REF_ROWS), :]
            total = total + jnp.dot(turned, x_ref[0, j], preferred_element_type=F32)
        acc_ref[...] = total
        return carry

    lax.fori_loop(0, PAIRS // 4, step, 0)

    @pl.when((n == pl.num_programs(0) - 1) & (me_ref[1] == 0))
    def _():
        keep_ref[...] = acc_ref[:, :HALF]
        send_ref[...] = acc_ref[:, HALF:]

    @pl.when((n == pl.num_programs(0) - 1) & (me_ref[1] == 1))
    def _():
        keep_ref[...] = acc_ref[:, HALF:]
        send_ref[...] = acc_ref[:, :HALF]


def flat_kernel(a_ref, b_ref, out_ref, sum_ref, lines_ref, grid_ref):
    sum_ref[:REF_ROWS] = a_ref[...] + b_ref[...]
    lane = lax.broadcasted_iota(jnp.int32, (CLS * 8, HALF), 1)
    for c in range(CLS):
        turns = sum_ref[pl.ds(c, HALF, stride=CLS), :]
        lines_ref[c] = turns.T
    for tile in range(GROUP // HALF):
        made = None
        for h in range(16):
            start = ROT * h - tile * HALF
            if start >= HALF or start + ROT <= 0:
                continue
            part = lines_ref[:, h * 8 : h * 8 + 8, :].reshape(CLS * 8, HALF)
            if start % HALF:
                part = pltpu.roll(part, start % HALF, 1)
            made = part if made is None else jnp.where(lane >= start, part, made)
        grid_ref[tile] = made
        for g in range(8):
            start = g * GROUP + tile * HALF
            out_ref[:, start : start + HALF] = grid_ref[tile, pl.ds(g, CLS, stride=8), :]


def gather_slots(block, holders):
    def swap(x, bits):
        return lax.ppermute(x, "cls", [(i, i ^ bits) for i in range(holders)])

    if holders == 8:
        r4 = swap(block, 4)
        r2 = swap(block, 2)
        r1 = swap(block, 1)
        r3 = swap(r2, 1)
        r6 = swap(r4, 2)
        r5 = swap(r4, 1)
        r7 = swap(r6, 1)
        return [x[None] for x in (block, r1, r2, r3, r4, r5, r6, r7)]
    slots = block[None]
    bits = 1
    while bits < holders:
        slots = jnp.concatenate([slots, swap(slots, bits)], axis=0)
        bits *= 2
    return [slots[s::SLOTS] for s in range(SLOTS)]


def per_device(particles, references, class_lists, offsets, inv_noise):
    holders = lax.axis_size("cls")
    nblocks = holders // SLOTS
    nbit = -(-holders * CLS // LANES)
    rows = ROWS + -(-(8 * nbit + 8) // 16) * 16
    vm = pl.BlockSpec(memory_space=pltpu.VMEM)
    sm = pl.BlockSpec(memory_space=pltpu.SMEM)
    params = pltpu.CompilerParams(vmem_limit_bytes=VMEM)
    me = jnp.stack([lax.axis_index("cls"), lax.axis_index("dom")]).astype(jnp.int32)

    def scratch(count):
        return [
            pltpu.VMEM((GROUP // HALF, count * 16, HALF), F32),
            pltpu.VMEM((count, 2, 16, 8, HALF), F32),
            pltpu.VMEM((2, ROT * count, HALF), F32),
        ]

    block = pl.pallas_call(
        lambda *a: particle_kernel(nbit, *a),
        out_shape=jax.ShapeDtypeStruct((rows, LANES), BF16),
        in_specs=[vm, vm, sm],
        out_specs=vm,
        scratch_shapes=scratch(PER_DEV),
        compiler_params=params,
        name="particle_turns",
    )(particles, class_lists, offsets)
    slots = gather_slots(block, holders)

    weights = jnp.repeat(inv_noise.reshape(8, 8).T, 2, axis=0).reshape(1, HALF)
    weights = jnp.concatenate([weights, weights], axis=1)
    refs = pl.pallas_call(
        reference_kernel,
        out_shape=jax.ShapeDtypeStruct((2 * REF_ROWS, LANES), BF16),
        in_specs=[vm, vm],
        out_specs=vm,
        scratch_shapes=scratch(CLS),
        compiler_params=params,
        name="reference_turns",
    )(references, weights)

    fx, fy = frequency_rows()
    full = lambda *shape: pl.BlockSpec(shape, lambda n, *_: (0,) * len(shape))
    images, expo, stat = pl.pallas_call(
        lambda *a: score_kernel(nbit, *a),
        out_shape=(
            jax.ShapeDtypeStruct((nblocks, PAIRS, LANES, LANES), BF16),
            jax.ShapeDtypeStruct((nblocks, REF_ROWS, LANES), F32),
            jax.ShapeDtypeStruct((nblocks, 8, HALF), F32),
        ),
        grid_spec=pltpu.PrefetchScalarGridSpec(
            num_scalar_prefetch=1,
            grid=(nblocks,),
            in_specs=[pl.BlockSpec((1, rows, LANES), lambda n, *_: (n, 0, 0))] * SLOTS
            + [full(ROWS, HALF), full(ROWS, HALF), full(2 * REF_ROWS, LANES)],
            out_specs=[
                pl.BlockSpec((1, PAIRS, LANES, LANES), lambda n, *_: (n, 0, 0, 0)),
                pl.BlockSpec((1, REF_ROWS, LANES), lambda n, *_: (n, 0, 0)),
                pl.BlockSpec((1, 8, HALF), lambda n, *_: (n, 0, 0)),
            ],
            scratch_shapes=[pltpu.VMEM((REF_ROWS, LANES), F32)],
        ),
        compiler_params=params,
        name="scores",
    )(me, *slots, jnp.asarray(fx), jnp.asarray(fy), refs)

    spread = pl.pallas_call(
        lambda *a: spread_kernel(holders, *a),
        out_shape=jax.ShapeDtypeStruct((holders, nblocks, 8, HALF), F32),
        in_specs=[sm, vm],
        out_specs=vm,
        compiler_params=params,
        name="spread",
    )(me, stat)
    got = lax.all_to_all(
        spread.reshape(holders, nblocks * 8, HALF), "cls", split_axis=0, concat_axis=0, tiled=True
    ).reshape(holders, nblocks, 8, HALF)

    keep, send, logs = pl.pallas_call(
        lambda *a: back_kernel(holders, *a),
        out_shape=(
            jax.ShapeDtypeStruct((REF_ROWS, HALF), F32),
            jax.ShapeDtypeStruct((REF_ROWS, HALF), F32),
            jax.ShapeDtypeStruct((8, HALF), F32),
        ),
        grid_spec=pltpu.PrefetchScalarGridSpec(
            num_scalar_prefetch=1,
            grid=(nblocks,),
            in_specs=[
                full(holders, nblocks, 8, HALF),
                pl.BlockSpec((1, 8, HALF), lambda n, *_: (n, 0, 0)),
                pl.BlockSpec((1, REF_ROWS, LANES), lambda n, *_: (n, 0, 0)),
                pl.BlockSpec((1, PAIRS, LANES, LANES), lambda n, *_: (n, 0, 0, 0)),
            ],
            out_specs=[full(REF_ROWS, HALF), full(REF_ROWS, HALF), full(8, HALF)],
            scratch_shapes=[pltpu.VMEM((2 * REF_ROWS, LANES), BF16), pltpu.VMEM((REF_ROWS, LANES), F32)],
        ),
        compiler_params=params,
        name="class_sums",
    )(me, got, stat, expo, images)

    other = lax.ppermute(send, "dom", [(0, 1), (1, 0)])
    sums = pl.pallas_call(
        flat_kernel,
        out_shape=jax.ShapeDtypeStruct((CLS, GROUP * 8), F32),
        in_specs=[vm, vm],
        out_specs=vm,
        scratch_shapes=[
            pltpu.VMEM((HALF * CLS, HALF), F32),
            pltpu.VMEM((CLS, HALF, HALF), F32),
            pltpu.VMEM((GROUP // HALF, CLS * 8, HALF), F32),
        ],
        compiler_params=params,
        name="flat_rows",
    )(keep, other)
    return sums, logs[0, :PER_DEV]


def solution(mesh):
    placed = (
        P(("groups", "cls", "dom"), None),
        P(("groups", "cls"), None),
        P(("groups", "cls", "dom"), None),
        P(("groups", "cls", "dom"), None, None),
        P(),
    )
    return jax.shard_map(
        per_device,
        mesh=mesh,
        in_specs=placed,
        out_specs=(P(("groups", "cls"), "dom"), P(("groups", "cls", "dom"))),
        check_vma=False,
    )
```

```python
import math

import jax
import jax.numpy as jnp
import numpy as np
from jax import lax
from jax.experimental import pallas as pl
from jax.experimental.pallas import tpu as pltpu
from jax.sharding import PartitionSpec as P

ROT = 72
CYCLES = 64
CLASS_LIST_SIZE = 32
BOX = 256
TRANS = 3
PER_DEV = 4
CLS = 8
SLOTS = 4
LANES = 256
HALF = 128
GROUP = 16 * ROT
ROWS = ROT * PER_DEV
REF_ROWS = ROT * CLS
STEPS = ROT // 4
HALF_TURN = ROWS // 2
CODED = 3 * 16
LOWEST = -1e30
VMEM = 20 * 1024 * 1024

F32 = jnp.float32
BF16 = jnp.bfloat16


def frequency_rows():
    row = lax.broadcasted_iota(jnp.int32, (HALF_TURN, HALF), 0)
    lane = lax.broadcasted_iota(jnp.int32, (HALF_TURN, HALF), 1)
    line = (lane % 8) * 16 + lane // 8
    radius = (line // 2 + 1).astype(F32) * (1.0 / BOX)
    angle = (2 * (row // PER_DEV) + line % 2).astype(F32) * (0.5 / ROT)
    c, s = cos_sin_turns(angle)
    return radius * c, radius * s


def half_turn_polynomials():
    t = np.cos(np.pi * (np.arange(400) + 0.5) / 400)
    z = (t + 1) / 8
    v = np.sqrt(z)
    sin_fit = np.polynomial.chebyshev.Chebyshev.fit(z, np.sin(np.pi * v) / v, 4, domain=[0, 0.25])
    cos_fit = np.polynomial.chebyshev.Chebyshev.fit(z, np.cos(np.pi * v), 5, domain=[0, 0.25])
    to_list = lambda f: [float(c) for c in f.convert(kind=np.polynomial.Polynomial).coef]
    return to_list(sin_fit), to_list(cos_fit)


SIN_COEF, COS_COEF = half_turn_polynomials()


def horner(coef, z):
    total = jnp.full_like(z, coef[-1])
    for c in coef[-2::-1]:
        total = total * z + c
    return total


def cos_sin_turns(u):
    v = u - jnp.round(u)
    z = v * v
    s = v * horner(SIN_COEF, z)
    c = horner(COS_COEF, z)
    s2 = s + s
    return 1.0 - s2 * s, s2 * c


def turn_major(x_ref, grid_ref, lines_ref, out_ref, count):
    for g in range(16):
        for tile in range(GROUP // HALF):
            start = g * GROUP + tile * HALF
            grid_ref[tile, pl.ds(g, count, stride=16), :] = x_ref[:, start : start + HALF].astype(F32)
    for h in range(16):
        tile, shift = divmod(ROT * h, HALF)
        if shift + ROT <= HALF:
            part = grid_ref[tile]
            if shift:
                part = pltpu.roll(part, HALF - shift, 1)
        else:
            part = jnp.concatenate([grid_ref[tile], grid_ref[tile + 1]], axis=1)
            part = pltpu.roll(part, LANES - shift, 1)[:, :HALF]
        lines_ref[:, :, h] = part.reshape(count, 2, 8, HALF)
    for p in range(count):
        for half in range(2):
            turns = lines_ref[p, half].reshape(HALF, HALF).T
            out_ref[half, pl.ds(p, ROT, stride=count), :] = turns[:ROT]


def particle_kernel(
    nbit, x_any, list_any, move_any, out_ref, x_ref, list_ref, move_ref, grid_ref, lines_ref, turns_ref, sems
):
    pairs = ((x_any, x_ref), (list_any, list_ref), (move_any, move_ref))
    copies = [pltpu.make_async_copy(a, b, sems.at[n]) for n, (a, b) in enumerate(pairs)]
    for copy in copies:
        copy.start()
    for copy in copies:
        copy.wait()
    turn_major(x_ref, grid_ref, lines_ref, turns_ref, PER_DEV)
    out_ref[:ROWS] = jnp.concatenate([turns_ref[0], turns_ref[1]], axis=1).astype(BF16)
    lists = list_ref[...]
    lane = lax.broadcasted_iota(jnp.int32, (PER_DEV, LANES), 1)
    parts = []
    for b in range(nbit):
        named = jnp.zeros((PER_DEV, LANES), F32)
        for j in range(CLASS_LIST_SIZE):
            named = jnp.where(lists[:, j : j + 1] == lane + b * LANES, 1.0, named)
        parts += [named, named]
    row = lax.broadcasted_iota(jnp.int32, (8, LANES), 0) % PER_DEV
    lane = lax.broadcasted_iota(jnp.int32, (8, LANES), 1)
    moves = jnp.zeros((8, LANES), F32)
    for p in range(PER_DEV):
        for t in range(TRANS):
            for a in range(2):
                here = (row == p) & (lane == 8 * a + t)
                moves = jnp.where(here, move_ref[t, a, p].astype(F32), moves)
    parts.append(moves)
    if nbit % 2 == 0:
        parts.append(jnp.zeros((8, LANES), F32))
    out_ref[ROWS:] = jnp.concatenate(parts, axis=0).astype(BF16)


def reference_kernel(x_ref, w_ref, out_ref, *rest):
    freq_refs, (grid_ref, lines_ref, turns_ref) = rest[:-3], rest[-3:]
    turn_major(x_ref, grid_ref, lines_ref, turns_ref, CLS)
    scaled = (jnp.concatenate([turns_ref[0], turns_ref[1]], axis=1) * w_ref[...]).astype(BF16)
    out_ref[:REF_ROWS] = scaled
    out_ref[REF_ROWS:] = scaled
    for ref, f in zip(freq_refs, frequency_rows()):
        ref[...] = f


def shift_kernel(nbit, block_ref, fx_ref, fy_ref, x_ref, bits_ref):
    first = ROWS + 16 * (nbit // 2)
    m = block_ref[0, first : first + 16].astype(F32)[8 * (nbit % 2) : 8 * (nbit % 2) + 8]
    m = jnp.concatenate([m, m], axis=0)
    moves = [
        (jnp.broadcast_to(m[:, t : t + 1], (16, HALF)), jnp.broadcast_to(m[:, 8 + t : 9 + t], (16, HALF)))
        for t in range(TRANS)
    ]
    bits_ref[0] = block_ref[0, ROWS : ROWS + bits_ref.shape[1]]

    def step(q, carry):
        rows = pl.ds(pl.multiple_of(q * 16, 16), 16)
        later = pl.ds(pl.multiple_of(q * 16, 16) + HALF_TURN, 16)
        fx = fx_ref[rows, :]
        fy = fy_ref[rows, :]
        near = block_ref[0, rows, :].astype(F32)
        far = block_ref[0, later, :].astype(F32)
        for t in range(TRANS):
            dx, dy = moves[t]
            c, s = cos_sin_turns(fx * dx + fy * dy)
            a, b = near[:, :HALF], near[:, HALF:]
            x_ref[0, q, t * 16 : t * 16 + 16, :HALF] = (a * c + b * s).astype(BF16)
            x_ref[0, q, t * 16 : t * 16 + 16, HALF:] = (b * c - a * s).astype(BF16)
            a, b = far[:, :HALF], far[:, HALF:]
            x_ref[0, q + STEPS // 2, t * 16 : t * 16 + 16, :HALF] = (a * c - b * s).astype(BF16)
            x_ref[0, q + STEPS // 2, t * 16 : t * 16 + 16, HALF:] = (b * c + a * s).astype(BF16)
        return carry

    lax.fori_loop(0, STEPS // 2, step, 0, unroll=3)


def xor_lanes(x, step):
    lane = lax.broadcasted_iota(jnp.int32, x.shape, x.ndim - 1)
    width = x.shape[-1]
    down = pltpu.roll(x, width - step, x.ndim - 1)
    up = pltpu.roll(x, step, x.ndim - 1)
    return jnp.where((lane // step) % 2 == 0, down, up)


def xor_slots(x, bits):
    if bits & 1:
        x = xor_lanes(x, 64)
    if bits & 2:
        x = xor_lanes(x, 128)
    return x


def images_of(x_refs, q):
    empty = jnp.zeros((16, LANES), BF16)
    return jnp.concatenate([v for x in x_refs for v in (x[0, q], empty)], axis=0)


def score_kernel(nbit, me_ref, *refs):
    x_refs = refs[:SLOTS]
    bit_refs = refs[SLOTS : 2 * SLOTS]
    own_ref, other_ref, e_ref, stat_ref, acc_ref = refs[2 * SLOTS :]
    acc_ref[...] = jnp.zeros_like(acc_ref)

    def step(g, carry):
        for side, ref in enumerate((own_ref, other_ref)):
            total = acc_ref[side, :REF_ROWS]
            for r in range(3):
                q = 3 * g + r
                turned = ref[pl.ds(pl.multiple_of(q * 32, 32), REF_ROWS), :]
                total += lax.dot_general(
                    turned, images_of(x_refs, q), (((1,), (1,)), ((), ())), preferred_element_type=F32
                )
            acc_ref[side, :REF_ROWS] = total
        return carry

    lax.fori_loop(0, STEPS // 3, step, 0)

    src = lax.broadcasted_iota(jnp.int32, (SLOTS * 16, LANES), 0)
    dst = lax.broadcasted_iota(jnp.int32, (SLOTS * 16, LANES), 1)
    ok = (src == dst // 64 * 16 + dst % 4) & (dst % 64 < 48) & (dst % 16 < 4)
    place = ok.astype(F32).astype(BF16)
    lane = lax.broadcasted_iota(jnp.int32, (CLS, LANES), 1)
    row = lax.broadcasted_iota(jnp.int32, (CLS, LANES), 0)
    top = jnp.full((CLS, LANES), LOWEST, F32)
    masks = []
    for side in range(2):
        chip = me_ref[0] ^ side
        named = jnp.zeros((CLS, SLOTS * 16), F32)
        for b in range(nbit):
            pick = (lane + b * LANES == chip * CLS + row).astype(F32).astype(BF16)
            first = 16 * (b // 2)
            bits = jnp.concatenate([r[0, first : first + 16] for r in bit_refs], axis=0)
            if b % 2:
                bits = jnp.concatenate(
                    [v for s in range(SLOTS) for v in (bits[s * 16 + 8 : s * 16 + 16], bits[s * 16 : s * 16 + 8])],
                    axis=0,
                )
            named += lax.dot_general(pick, bits, (((1,), (1,)), ((), ())), preferred_element_type=F32)
        mask = jnp.dot(named.astype(BF16), place, preferred_element_type=F32) > 0.5
        masks.append(mask)
        acc_ref[side, REF_ROWS:] = acc_ref[side, :32]

        def body_max(i, top, side=side, mask=mask):
            at = lambda d: acc_ref[side, pl.ds(pl.multiple_of((i + d) * 8, 8), 8), :]
            s = at(0)
            for d in range(1, 4):
                s += pltpu.roll(at(d), LANES - 4 * d, 1)
            s = jnp.where(mask, s, LOWEST)
            e_ref[0, side, pl.ds(pl.multiple_of(i * 8, 8), 8), :] = s
            return jnp.maximum(top, s)

        top = lax.fori_loop(0, ROT, body_max, top, unroll=8)
    top = jnp.broadcast_to(jnp.max(top, axis=0, keepdims=True), (CLS, LANES))
    top = jnp.maximum(top, xor_lanes(top, 16))
    top = jnp.maximum(top, xor_lanes(top, 32))
    total = jnp.zeros((CLS, LANES), F32)
    for side in range(2):

        def body_exp(i, total, side=side):
            rows = pl.ds(pl.multiple_of(i * 8, 8), 8)
            e = jnp.where(masks[side], jnp.exp(e_ref[0, side, rows, :] - top), 0.0)
            e_ref[0, side, rows, :] = e
            return total + e

        total = lax.fori_loop(0, ROT, body_exp, total, unroll=8)
    total = jnp.broadcast_to(jnp.sum(total, axis=0, keepdims=True), (CLS, LANES))
    total = total + xor_lanes(total, 16)
    total = total + xor_lanes(total, 32)
    stat_ref[0] = jnp.where(row == 0, top, total)


def back_kernel(side, nblocks, me_ref, *refs):
    got_refs = refs[:SLOTS]
    stat_ref, e_ref = refs[SLOTS : SLOTS + 2]
    x_refs = refs[SLOTS + 2 : 2 * SLOTS + 2]
    keep_ref, send_ref, *log_ref = refs[2 * SLOTS + 2 : -2]
    w_ref, acc_ref = refs[-2:]
    n = pl.program_id(0) if nblocks > 1 else 0
    stats = [
        xor_slots(got_refs[low][high, n ^ high], low) for high in range(nblocks) for low in range(SLOTS)
    ]
    spread = lambda x, r: jnp.broadcast_to(x[r : r + 1], (8, LANES))
    tops = [spread(x, 0) for x in stats]
    best = tops[0]
    for top in tops[1:]:
        best = jnp.maximum(best, top)
    evidence = jnp.zeros((8, LANES), F32)
    for top, x in zip(tops, stats):
        evidence = evidence + spread(x, 1) * jnp.exp(top - best)
    lane = lax.broadcasted_iota(jnp.int32, (8, LANES), 1)
    live = (lane % 64 < 48) & (lane % 16 < 4)
    factor = jnp.where(live, jnp.exp(spread(stat_ref[0], 0) - best) / evidence, 0.0)

    def start():
        acc_ref[...] = jnp.zeros_like(acc_ref)
        if log_ref:
            log_ref[0][...] = best + jnp.log(evidence)

    if nblocks > 1:
        pl.when(n == 0)(start)
    else:
        start()

    def weights(i):
        i = i % ROT
        return e_ref[0, side, i * 8 : i * 8 + 8, :] * factor

    window = [weights(i) for i in (-3, -2, -1)]
    for i in range(0, ROT, 2):
        rows = []
        for d in range(2):
            now = weights(i + d)
            a, b, c = window
            rows.append(now + pltpu.roll(c, 4, 1) + pltpu.roll(b, 8, 1) + pltpu.roll(a, 12, 1))
            window = [b, c, now]
        pair = jnp.concatenate(rows, axis=0).astype(BF16)
        w_ref[i * 8 : i * 8 + 16, :] = pair
        w_ref[REF_ROWS + i * 8 : REF_ROWS + i * 8 + 16, :] = pair

    def step(g, carry):
        total = acc_ref[...]
        for r in range(3):
            q = 3 * g + r
            turned = w_ref[pl.ds(pl.multiple_of((STEPS - q) * 32, 32), REF_ROWS), :]
            total += jnp.dot(turned, images_of(x_refs, q), preferred_element_type=F32)
        acc_ref[...] = total
        return carry

    lax.fori_loop(0, STEPS // 3, step, 0)

    @pl.when((n == nblocks - 1) & (me_ref[1] == 0))
    def _():
        keep_ref[...] = acc_ref[:, :HALF]
        send_ref[...] = acc_ref[:, HALF:]

    @pl.when((n == nblocks - 1) & (me_ref[1] == 1))
    def _():
        keep_ref[...] = acc_ref[:, HALF:]
        send_ref[...] = acc_ref[:, :HALF]


def flat_kernel(a_ref, b_ref, c_ref, out_ref, sum_ref, lines_ref, grid_ref):
    sum_ref[:REF_ROWS] = a_ref[...] + b_ref[...] + c_ref[...].astype(F32)
    lane = lax.broadcasted_iota(jnp.int32, (CLS * 8, HALF), 1)
    for c in range(CLS):
        turns = sum_ref[pl.ds(c, HALF, stride=CLS), :]
        lines_ref[c] = turns.T
    for tile in range(GROUP // HALF):
        made = None
        for h in range(16):
            start = ROT * h - tile * HALF
            if start >= HALF or start + ROT <= 0:
                continue
            part = lines_ref[:, h * 8 : h * 8 + 8, :].reshape(CLS * 8, HALF)
            if start % HALF:
                part = pltpu.roll(part, start % HALF, 1)
            made = part if made is None else jnp.where(lane >= start, part, made)
        grid_ref[tile] = made
        for g in range(8):
            start = g * GROUP + tile * HALF
            out_ref[:, start : start + HALF] = grid_ref[tile, pl.ds(g, CLS, stride=8), :]


def swap(x, axis, bits):
    return lax.ppermute(x, axis, [(i, i ^ bits) for i in range(lax.axis_size(axis))])


def gather_slots(block, relay):
    if lax.axis_size("cls") == 2 * SLOTS:
        r2 = swap(block, "cls", 4)
        r1 = swap(block, "cls", 2)
        r3 = swap(r2, "cls", 2) if relay else swap(block, "cls", 6)
        return [x[None] for x in (block, r1, r2, r3)]
    slots = block[None]
    bits = 2
    while bits < lax.axis_size("cls"):
        slots = jnp.concatenate([slots, swap(slots, "cls", bits)], axis=0)
        bits *= 2
    return [slots[s::SLOTS] for s in range(SLOTS)]


def call(name, body, nblocks, inputs, outputs, scratch):
    def spec(shape, kind):
        if kind == "scalar":
            return pl.BlockSpec(memory_space=pltpu.SMEM)
        if kind == "any":
            return pl.BlockSpec(memory_space=pl.ANY)
        if nblocks == 1:
            return pl.BlockSpec(memory_space=pltpu.VMEM)
        rest = (0,) * (len(shape) - 1)
        if kind == "block":
            return pl.BlockSpec((1,) + shape[1:], lambda n: (n,) + rest)
        return pl.BlockSpec(shape, lambda n: (0,) + rest)

    grid = {"grid": (nblocks,)} if nblocks > 1 else {}
    return pl.pallas_call(
        body,
        out_shape=tuple(jax.ShapeDtypeStruct(shape, dtype) for shape, dtype, _ in outputs),
        in_specs=[spec(x.shape, kind) for x, kind in inputs],
        out_specs=tuple(spec(shape, kind) for shape, _, kind in outputs),
        scratch_shapes=scratch,
        compiler_params=pltpu.CompilerParams(vmem_limit_bytes=VMEM),
        name=name,
        **grid,
    )(*[x for x, _ in inputs])


def per_device(particles, references, class_lists, offsets, inv_noise):
    holders = lax.axis_size("cls")
    nblocks = holders // 2 // SLOTS
    nbit = -(-holders * CLS // LANES)
    extra = -(-(8 * nbit + 8) // 16) * 16
    rows = ROWS + extra
    me = jnp.stack([lax.axis_index("cls"), lax.axis_index("dom")]).astype(jnp.int32)

    def scratch(count):
        return [
            pltpu.VMEM((GROUP // HALF, count * 16, HALF), F32),
            pltpu.VMEM((count, 2, 16, 8, HALF), F32),
            pltpu.VMEM((2, ROT * count, HALF), F32),
        ]

    moves = jnp.transpose(offsets, (1, 2, 0))
    (block,) = call(
        "particle_turns",
        lambda *a: particle_kernel(nbit, *a),
        1,
        [(particles, "any"), (class_lists, "any"), (moves, "any")],
        [((rows, LANES), BF16, "all")],
        [
            pltpu.VMEM(particles.shape, BF16),
            pltpu.VMEM(class_lists.shape, jnp.int32),
            pltpu.SMEM(moves.shape, jnp.int32),
        ]
        + scratch(PER_DEV)
        + [pltpu.SemaphoreType.DMA((3,))],
    )
    slots = gather_slots(block, True)
    far_references = swap(references, "cls", 1)

    weights = jnp.repeat(inv_noise.reshape(8, 8).T, 2, axis=0).reshape(1, HALF)
    weights = jnp.concatenate([weights, weights], axis=1)
    turned = ((2 * REF_ROWS, LANES), BF16, "all")
    freq = ((HALF_TURN, HALF), F32, "all")
    own_refs, fx, fy = call(
        "own_references", reference_kernel, 1, [(references, "all"), (weights, "all")], [turned, freq, freq], scratch(CLS)
    )
    (far_refs,) = call(
        "far_references", reference_kernel, 1, [(far_references, "all"), (weights, "all")], [turned], scratch(CLS)
    )

    bit_rows = 16 * -(-nbit // 2)
    images, bits = [], []
    for slot in slots:
        x, b = call(
            "shifted",
            lambda *a: shift_kernel(nbit, *a),
            nblocks,
            [(slot, "block"), (fx, "all"), (fy, "all")],
            [((nblocks, STEPS, CODED, LANES), BF16, "block"), ((nblocks, bit_rows, LANES), BF16, "block")],
            [],
        )
        images.append(x)
        bits.append(b)

    expo, stat = call(
        "scores",
        lambda *a: score_kernel(nbit, *a),
        nblocks,
        [(me, "scalar")] + [(x, "block") for x in images + bits] + [(own_refs, "all"), (far_refs, "all")],
        [((nblocks, 2, REF_ROWS, LANES), F32, "block"), ((nblocks, 8, LANES), F32, "block")],
        [pltpu.VMEM((2, REF_ROWS + 32, LANES), F32)],
    )
    got = gather_slots(stat, False)

    def back(side):
        half = ((REF_ROWS, HALF), F32, "all")
        return call(
            "far_sums" if side else "own_sums",
            lambda *a: back_kernel(side, nblocks, *a),
            nblocks,
            [(me, "scalar")] + [(g, "all") for g in got] + [(stat, "block"), (expo, "block")] + [(x, "block") for x in images],
            [half, half] + [((8, LANES), F32, "all")] * side,
            [pltpu.VMEM((2 * REF_ROWS, LANES), BF16), pltpu.VMEM((REF_ROWS, LANES), F32)],
        )

    far_keep, far_send, logs = back(1)
    far_got = swap(far_send, "dom", 1)
    keep, send = back(0)
    own_got = swap(send, "dom", 1)
    far_sum = swap((far_keep + far_got).astype(BF16), "cls", 1)
    (sums,) = call(
        "flat_rows",
        flat_kernel,
        1,
        [(keep, "all"), (own_got, "all"), (far_sum, "all")],
        [((CLS, GROUP * 8), F32, "all")],
        [
            pltpu.VMEM((HALF * CLS, HALF), F32),
            pltpu.VMEM((CLS, HALF, HALF), F32),
            pltpu.VMEM((GROUP // HALF, CLS * 8, HALF), F32),
        ],
    )
    return sums, logs[0, :PER_DEV]


def solution(mesh):
    placed = (
        P(("groups", "cls", "dom"), None),
        P(("groups", "cls"), None),
        P(("groups", "cls", "dom"), None),
        P(("groups", "cls", "dom"), None, None),
        P(),
    )
    return jax.shard_map(
        per_device,
        mesh=mesh,
        in_specs=placed,
        out_specs=(P(("groups", "cls"), "dom"), P(("groups", "cls", "dom"))),
        check_vma=False,
    )
```

```python
import math

import jax
import jax.numpy as jnp
import numpy as np
from jax import lax
from jax.experimental import pallas as pl
from jax.experimental.pallas import tpu as pltpu
from jax.sharding import PartitionSpec as P

ROT = 72
CYCLES = 64
CLASS_LIST_SIZE = 32
BOX = 256
TRANS = 3
PER_DEV = 4
CLS = 8
SLOTS = 4
LANES = 256
HALF = 128
GROUP = 16 * ROT
ROWS = ROT * PER_DEV
REF_ROWS = ROT * CLS
STEPS = ROT // 4
HALF_TURN = ROWS // 2
CODED = 3 * 16
LOWEST = -1e30
VMEM = 20 * 1024 * 1024

F32 = jnp.float32
BF16 = jnp.bfloat16


def frequency_rows():
    row = lax.broadcasted_iota(jnp.int32, (HALF_TURN, HALF), 0)
    lane = lax.broadcasted_iota(jnp.int32, (HALF_TURN, HALF), 1)
    line = (lane % 8) * 16 + lane // 8
    radius = (line // 2 + 1).astype(F32) * (1.0 / BOX)
    angle = (2 * (row // PER_DEV) + line % 2).astype(F32) * (0.5 / ROT)
    c, s = cos_sin_turns(angle)
    return radius * c, radius * s


def half_turn_polynomials():
    t = np.cos(np.pi * (np.arange(400) + 0.5) / 400)
    z = (t + 1) / 8
    v = np.sqrt(z)
    sin_fit = np.polynomial.chebyshev.Chebyshev.fit(z, np.sin(np.pi * v) / v, 4, domain=[0, 0.25])
    cos_fit = np.polynomial.chebyshev.Chebyshev.fit(z, np.cos(np.pi * v), 5, domain=[0, 0.25])
    to_list = lambda f: [float(c) for c in f.convert(kind=np.polynomial.Polynomial).coef]
    return to_list(sin_fit), to_list(cos_fit)


SIN_COEF, COS_COEF = half_turn_polynomials()


def horner(coef, z):
    total = jnp.full_like(z, coef[-1])
    for c in coef[-2::-1]:
        total = total * z + c
    return total


def cos_sin_turns(u):
    v = u - jnp.round(u)
    z = v * v
    s = v * horner(SIN_COEF, z)
    c = horner(COS_COEF, z)
    s2 = s + s
    return 1.0 - s2 * s, s2 * c


def turn_major(x_ref, grid_ref, lines_ref, out_ref, count):
    for g in range(16):
        for tile in range(GROUP // HALF):
            start = g * GROUP + tile * HALF
            grid_ref[tile, pl.ds(g, count, stride=16), :] = x_ref[:, start : start + HALF].astype(F32)
    for h in range(16):
        tile, shift = divmod(ROT * h, HALF)
        if shift + ROT <= HALF:
            part = grid_ref[tile]
            if shift:
                part = pltpu.roll(part, HALF - shift, 1)
        else:
            part = jnp.concatenate([grid_ref[tile], grid_ref[tile + 1]], axis=1)
            part = pltpu.roll(part, LANES - shift, 1)[:, :HALF]
        lines_ref[:, :, h] = part.reshape(count, 2, 8, HALF)
    for p in range(count):
        for half in range(2):
            turns = lines_ref[p, half].reshape(HALF, HALF).T
            out_ref[half, pl.ds(p, ROT, stride=count), :] = turns[:ROT]


def particle_kernel(
    nbit, x_any, list_any, move_any, out_ref, x_ref, list_ref, move_ref, grid_ref, lines_ref, turns_ref, sems
):
    pairs = ((x_any, x_ref), (list_any, list_ref), (move_any, move_ref))
    copies = [pltpu.make_async_copy(a, b, sems.at[n]) for n, (a, b) in enumerate(pairs)]
    for copy in copies:
        copy.start()
    copies[0].wait()
    turn_major(x_ref, grid_ref, lines_ref, turns_ref, PER_DEV)
    out_ref[:ROWS] = jnp.concatenate([turns_ref[0], turns_ref[1]], axis=1).astype(BF16)
    copies[1].wait()
    copies[2].wait()
    lists = list_ref[...]
    lane = lax.broadcasted_iota(jnp.int32, (PER_DEV, LANES), 1)
    parts = []
    for b in range(nbit):
        named = jnp.zeros((PER_DEV, LANES), F32)
        for j in range(CLASS_LIST_SIZE):
            named = jnp.where(lists[:, j : j + 1] == lane + b * LANES, 1.0, named)
        parts += [named, named]
    row = lax.broadcasted_iota(jnp.int32, (8, LANES), 0) % PER_DEV
    lane = lax.broadcasted_iota(jnp.int32, (8, LANES), 1)
    moves = jnp.zeros((8, LANES), F32)
    for p in range(PER_DEV):
        for t in range(TRANS):
            for a in range(2):
                here = (row == p) & (lane == 8 * a + t)
                moves = jnp.where(here, move_ref[t, a, p].astype(F32), moves)
    parts.append(moves)
    if nbit % 2 == 0:
        parts.append(jnp.zeros((8, LANES), F32))
    out_ref[ROWS:] = jnp.concatenate(parts, axis=0).astype(BF16)


def reference_kernel(x_ref, w_ref, out_ref, *rest):
    freq_refs, (grid_ref, lines_ref, turns_ref) = rest[:-3], rest[-3:]
    turn_major(x_ref, grid_ref, lines_ref, turns_ref, CLS)
    scaled = (jnp.concatenate([turns_ref[0], turns_ref[1]], axis=1) * w_ref[...]).astype(BF16)
    out_ref[:REF_ROWS] = scaled
    out_ref[REF_ROWS:] = scaled
    for ref, f in zip(freq_refs, frequency_rows()):
        ref[...] = f


def shift_kernel(nbit, block_ref, fx_ref, fy_ref, x_ref, bits_ref):
    first = ROWS + 16 * (nbit // 2)
    m = block_ref[0, first : first + 16].astype(F32)[8 * (nbit % 2) : 8 * (nbit % 2) + 8]
    m = jnp.concatenate([m, m], axis=0)
    moves = [
        (jnp.broadcast_to(m[:, t : t + 1], (16, HALF)), jnp.broadcast_to(m[:, 8 + t : 9 + t], (16, HALF)))
        for t in range(TRANS)
    ]
    bits_ref[0] = block_ref[0, ROWS : ROWS + bits_ref.shape[1]]

    def step(q, carry):
        rows = pl.ds(pl.multiple_of(q * 16, 16), 16)
        later = pl.ds(pl.multiple_of(q * 16, 16) + HALF_TURN, 16)
        fx = fx_ref[rows, :]
        fy = fy_ref[rows, :]
        near = block_ref[0, rows, :].astype(F32)
        far = block_ref[0, later, :].astype(F32)
        for t in range(TRANS):
            dx, dy = moves[t]
            c, s = cos_sin_turns(fx * dx + fy * dy)
            a, b = near[:, :HALF], near[:, HALF:]
            x_ref[0, q, t * 16 : t * 16 + 16, :HALF] = (a * c + b * s).astype(BF16)
            x_ref[0, q, t * 16 : t * 16 + 16, HALF:] = (b * c - a * s).astype(BF16)
            a, b = far[:, :HALF], far[:, HALF:]
            x_ref[0, q + STEPS // 2, t * 16 : t * 16 + 16, :HALF] = (a * c - b * s).astype(BF16)
            x_ref[0, q + STEPS // 2, t * 16 : t * 16 + 16, HALF:] = (b * c + a * s).astype(BF16)
        return carry

    lax.fori_loop(0, STEPS // 2, step, 0, unroll=3)


def xor_lanes(x, step):
    lane = lax.broadcasted_iota(jnp.int32, x.shape, x.ndim - 1)
    width = x.shape[-1]
    down = pltpu.roll(x, width - step, x.ndim - 1)
    up = pltpu.roll(x, step, x.ndim - 1)
    return jnp.where((lane // step) % 2 == 0, down, up)


def xor_slots(x, bits):
    if bits & 1:
        x = xor_lanes(x, 64)
    if bits & 2:
        x = xor_lanes(x, 4)
    return x


def live_lanes(shape):
    lane = lax.broadcasted_iota(jnp.int32, shape, 1)
    return (lane % 64 < 16 * TRANS) & (lane % 16 < 8)


def images_of(x_refs, q):
    empty = jnp.zeros((16, LANES), BF16)
    return jnp.concatenate([v for x in x_refs for v in (x[0, q], empty)], axis=0)


def score_kernel(nbit, me_ref, *refs):
    x_refs = refs[:SLOTS]
    bit_refs = refs[SLOTS : 2 * SLOTS]
    own_ref, far_ref, e_ref, stat_ref, acc_ref, pair_ref = refs[2 * SLOTS :]

    src = lax.broadcasted_iota(jnp.int32, (SLOTS * 16, HALF), 0)
    dst = lax.broadcasted_iota(jnp.int32, (SLOTS * 16, HALF), 1)
    slot = dst // 64 + 2 * (dst % 16 // 4)
    place = ((src == slot * 16 + dst % 4) & live_lanes(src.shape)).astype(F32).astype(BF16)
    lane = lax.broadcasted_iota(jnp.int32, (CLS, LANES), 1)
    row = lax.broadcasted_iota(jnp.int32, (CLS, LANES), 0)
    turn = lax.broadcasted_iota(jnp.int32, (CLS, HALF), 1) % 16 // 4
    images = jnp.concatenate([images_of(x_refs, q) for q in range(STEPS)], axis=1)
    top = jnp.full((CLS, HALF), LOWEST, F32)
    for side, ref in enumerate((own_ref, far_ref)):
        turned = jnp.concatenate([ref[q * 32 : q * 32 + REF_ROWS] for q in range(STEPS)], axis=1)
        acc_ref[...] = lax.dot_general(turned, images, (((1,), (1,)), ((), ())), preferred_element_type=F32)

        named = jnp.zeros((CLS, SLOTS * 16), F32)
        chip = me_ref[0] ^ side
        for b in range(nbit):
            pick = (lane + b * LANES == chip * CLS + row).astype(F32).astype(BF16)
            first = 16 * (b // 2)
            bits = jnp.concatenate([r[0, first : first + 16] for r in bit_refs], axis=0)
            if b % 2:
                bits = jnp.concatenate(
                    [v for s in range(SLOTS) for v in (bits[s * 16 + 8 : s * 16 + 16], bits[s * 16 : s * 16 + 8])],
                    axis=0,
                )
            named += lax.dot_general(pick, bits, (((1,), (1,)), ((), ())), preferred_element_type=F32)
        mask = jnp.dot(named.astype(BF16), place, preferred_element_type=F32) > 0.5

        def at(i):
            i = i % ROT
            return acc_ref[i * 8 : i * 8 + 8, :HALF], acc_ref[i * 8 : i * 8 + 8, HALF:]

        for i in range(ROT):
            (a, b), (c, d) = at(i), at(i + 1)
            low = a + pltpu.roll(c, HALF - 4, 1)
            high = b + pltpu.roll(d, HALF - 4, 1)
            pair_ref[i * 8 : i * 8 + 8] = jnp.where(turn % 2 == 0, low, pltpu.roll(high, 4, 1))
        for i in range(ROT):
            n = (i + 2) % ROT
            s = pair_ref[i * 8 : i * 8 + 8] + pltpu.roll(pair_ref[n * 8 : n * 8 + 8], HALF - 8, 1)
            s = jnp.where(mask, s, LOWEST)
            e_ref[0, side, i * 8 : i * 8 + 8] = s
            top = jnp.maximum(top, s)
    top = jnp.broadcast_to(jnp.max(top, axis=0, keepdims=True), (CLS, HALF))
    top = jnp.maximum(top, xor_lanes(top, 16))
    top = jnp.maximum(top, xor_lanes(top, 32))
    base = jnp.where(top == LOWEST, 0.0, top)
    total = jnp.zeros((CLS, HALF), F32)
    for side in range(2):
        for i in range(ROT):
            e = jnp.exp(e_ref[0, side, i * 8 : i * 8 + 8] - base)
            e_ref[0, side, i * 8 : i * 8 + 8] = e
            total += e
    total = jnp.broadcast_to(jnp.sum(total, axis=0, keepdims=True), (CLS, HALF))
    total = total + xor_lanes(total, 16)
    total = total + xor_lanes(total, 32)
    stat_ref[0] = jnp.where(lax.broadcasted_iota(jnp.int32, (CLS, HALF), 0) == 0, top, total)


def factors(got_refs, stat_ref, nblocks, n):
    stats = [
        xor_slots(got_refs[low][high, n ^ high], low) for high in range(nblocks) for low in range(SLOTS)
    ]
    spread = lambda x, r: jnp.broadcast_to(x[r : r + 1], (8, HALF))
    tops = [spread(x, 0) for x in stats]
    best = tops[0]
    for top in tops[1:]:
        best = jnp.maximum(best, top)
    evidence = jnp.zeros((8, HALF), F32)
    for top, x in zip(tops, stats):
        evidence = evidence + spread(x, 1) * jnp.exp(top - best)
    factor = jnp.where(live_lanes((8, HALF)), jnp.exp(spread(stat_ref[0], 0) - best) / evidence, 0.0)
    return factor, best + jnp.log(evidence)


def spread_kernel(e_ref, far_ref, own_ref):
    turn = lax.broadcasted_iota(jnp.int32, (8, HALF), 1) % 16 // 4
    for side, out_ref in enumerate((own_ref, far_ref)):

        def weights(i):
            i = i % ROT
            w = e_ref[0, side, i * 8 : i * 8 + 8]
            return jnp.where(turn == 0, w, 0.0), jnp.where(turn == 1, w, 0.0)

        def two_turns(now, before):
            return now[0] + pltpu.roll(before[0], 4, 1), pltpu.roll(now[1], HALF - 4, 1) + before[1]

        plain = [weights(i) for i in (-3, -2, -1)]
        pairs = [two_turns(plain[1], plain[0]), two_turns(plain[2], plain[1])]
        before = plain[2]
        for i in range(ROT):
            now = weights(i)
            pairs.append(two_turns(now, before))
            before = now
            last = pairs.pop(0)
            (a, b), (c, d) = pairs[-1], last
            out_ref[0, i * 8 : i * 8 + 8, :HALF] = a + pltpu.roll(c, 8, 1)
            out_ref[0, i * 8 : i * 8 + 8, HALF:] = b + pltpu.roll(d, 8, 1)


def back_kernel(nblocks, me_ref, *refs):
    got_refs = refs[:SLOTS]
    stat_ref, e_ref = refs[SLOTS : SLOTS + 2]
    x_refs = refs[SLOTS + 2 : 2 * SLOTS + 2]
    keep_ref, send_ref, *log_ref = refs[2 * SLOTS + 2 : -2]
    w_ref, acc_ref = refs[-2:]
    n = pl.program_id(0) if nblocks > 1 else 0
    factor, logs = factors(got_refs, stat_ref, nblocks, n)
    if log_ref:

        @pl.when(n == 0)
        def _():
            log_ref[0][...] = logs

    turn = lax.broadcasted_iota(jnp.int32, (8, HALF), 1) % 16 // 4
    low = jnp.where(turn == 0, factor, 0.0)
    high = pltpu.roll(jnp.where(turn == 1, factor, 0.0), HALF - 4, 1)
    low, high = (f + pltpu.roll(f, 4, 1) for f in (low, high))
    low, high = (f + pltpu.roll(f, 8, 1) for f in (low, high))
    both = jnp.concatenate([low, high], axis=1)
    both = jnp.concatenate([both, both], axis=0)
    for i in range(0, REF_ROWS, 16):
        pair = (e_ref[0, i : i + 16] * both).astype(BF16)
        w_ref[i : i + 16] = pair
        w_ref[REF_ROWS + i : REF_ROWS + i + 16] = pair

    turned = jnp.concatenate(
        [w_ref[(STEPS - q) * 32 : (STEPS - q) * 32 + REF_ROWS] for q in range(STEPS)], axis=1
    )
    images = jnp.concatenate([images_of(x_refs, q) for q in range(STEPS)], axis=0)
    made = jnp.dot(turned, images, preferred_element_type=F32)
    if nblocks == 1:
        acc_ref[...] = made
    else:

        @pl.when(n == 0)
        def _():
            acc_ref[...] = made

        @pl.when(n > 0)
        def _():
            acc_ref[...] += made

    @pl.when((n == nblocks - 1) & (me_ref[1] == 0))
    def _():
        keep_ref[...] = acc_ref[:, :HALF]
        send_ref[...] = acc_ref[:, HALF:]

    @pl.when((n == nblocks - 1) & (me_ref[1] == 1))
    def _():
        keep_ref[...] = acc_ref[:, HALF:]
        send_ref[...] = acc_ref[:, :HALF]


def flat_kernel(a_ref, b_ref, c_ref, out_ref, sum_ref, lines_ref, grid_ref):
    sum_ref[:REF_ROWS] = a_ref[...] + b_ref[...] + c_ref[...].astype(F32)
    lane = lax.broadcasted_iota(jnp.int32, (CLS * 8, HALF), 1)
    for c in range(CLS):
        turns = sum_ref[pl.ds(c, HALF, stride=CLS), :]
        lines_ref[c] = turns.T
    for tile in range(GROUP // HALF):
        made = None
        for h in range(16):
            start = ROT * h - tile * HALF
            if start >= HALF or start + ROT <= 0:
                continue
            part = lines_ref[:, h * 8 : h * 8 + 8, :].reshape(CLS * 8, HALF)
            if start % HALF:
                part = pltpu.roll(part, start % HALF, 1)
            made = part if made is None else jnp.where(lane >= start, part, made)
        grid_ref[tile] = made
        for g in range(8):
            start = g * GROUP + tile * HALF
            out_ref[:, start : start + HALF] = grid_ref[tile, pl.ds(g, CLS, stride=8), :]


def swap(x, axis, bits):
    return lax.ppermute(x, axis, [(i, i ^ bits) for i in range(lax.axis_size(axis))])


def gather_slots(block, relay):
    if lax.axis_size("cls") == 2 * SLOTS:
        r2 = swap(block, "cls", 4)
        r1 = swap(block, "cls", 2)
        r3 = swap(r2, "cls", 2) if relay else swap(block, "cls", 6)
        return [x[None] for x in (block, r1, r2, r3)]
    slots = block[None]
    bits = 2
    while bits < lax.axis_size("cls"):
        slots = jnp.concatenate([slots, swap(slots, "cls", bits)], axis=0)
        bits *= 2
    return [slots[s::SLOTS] for s in range(SLOTS)]


def call(name, body, nblocks, inputs, outputs, scratch, micros=1, vmem=VMEM):
    def spec(shape, kind):
        if kind == "scalar":
            return pl.BlockSpec(memory_space=pltpu.SMEM)
        if kind == "any":
            return pl.BlockSpec(memory_space=pltpu.HBM)
        if nblocks == 1:
            return pl.BlockSpec(memory_space=pltpu.VMEM)
        rest = (0,) * (len(shape) - 1)
        if kind == "block":
            return pl.BlockSpec((1,) + shape[1:], lambda n: (n,) + rest)
        return pl.BlockSpec(shape, lambda n: (0,) + rest)

    grid = {"grid": (nblocks,)} if nblocks > 1 else {}
    return pl.pallas_call(
        body,
        out_shape=tuple(jax.ShapeDtypeStruct(shape, dtype) for shape, dtype, _ in outputs),
        in_specs=[spec(x.shape, kind) for x, kind in inputs],
        out_specs=tuple(spec(shape, kind) for shape, _, kind in outputs),
        scratch_shapes=scratch,
        compiler_params=pltpu.CompilerParams(vmem_limit_bytes=vmem),
        cost_estimate=pl.CostEstimate(flops=micros * 10**9, bytes_accessed=micros * 10**6, transcendentals=0),
        name=name,
        **grid,
    )(*[x for x, _ in inputs])


def per_device(particles, references, class_lists, offsets, inv_noise):
    holders = lax.axis_size("cls")
    nblocks = holders // 2 // SLOTS
    nbit = -(-holders * CLS // LANES)
    extra = -(-(8 * nbit + 8) // 16) * 16
    rows = ROWS + extra
    me = jnp.stack([lax.axis_index("cls"), lax.axis_index("dom")]).astype(jnp.int32)

    def scratch(count):
        return [
            pltpu.VMEM((GROUP // HALF, count * 16, HALF), F32),
            pltpu.VMEM((count, 2, 16, 8, HALF), F32),
            pltpu.VMEM((2, ROT * count, HALF), F32),
        ]

    moves = jnp.transpose(offsets, (1, 2, 0))
    (block,) = call(
        "particle_turns",
        lambda *a: particle_kernel(nbit, *a),
        1,
        [(particles, "any"), (class_lists, "any"), (moves, "any")],
        [((rows, LANES), BF16, "all")],
        [
            pltpu.VMEM(particles.shape, BF16),
            pltpu.VMEM(class_lists.shape, jnp.int32),
            pltpu.SMEM(moves.shape, jnp.int32),
        ]
        + scratch(PER_DEV)
        + [pltpu.SemaphoreType.DMA((3,))],
        vmem=60 * 1024 * 1024,
    )
    slots = gather_slots(block, True)
    far_references = swap(references, "cls", 1)

    weights = jnp.repeat(inv_noise.reshape(8, 8).T, 2, axis=0).reshape(1, HALF)
    weights = jnp.concatenate([weights, weights], axis=1)
    turned = ((2 * REF_ROWS, LANES), BF16, "all")
    freq = ((HALF_TURN, HALF), F32, "all")
    own_refs, fx, fy = call(
        "own_references", reference_kernel, 1, [(references, "all"), (weights, "all")], [turned, freq, freq], scratch(CLS)
    )
    (far_refs,) = call(
        "far_references", reference_kernel, 1, [(far_references, "all"), (weights, "all")], [turned], scratch(CLS)
    )

    bit_rows = 16 * -(-nbit // 2)
    images, bits = [], []
    for slot in slots:
        x, b = call(
            "shifted",
            lambda *a: shift_kernel(nbit, *a),
            nblocks,
            [(slot, "block"), (fx, "all"), (fy, "all")],
            [((nblocks, STEPS, CODED, LANES), BF16, "block"), ((nblocks, bit_rows, LANES), BF16, "block")],
            [],
        )
        images.append(x)
        bits.append(b)

    expo, stat = call(
        "scores",
        lambda *a: score_kernel(nbit, *a),
        nblocks,
        [(me, "scalar")] + [(x, "block") for x in images + bits] + [(own_refs, "all"), (far_refs, "all")],
        [((nblocks, 2, REF_ROWS, HALF), F32, "block"), ((nblocks, 8, HALF), F32, "block")],
        [pltpu.VMEM((REF_ROWS, LANES), F32), pltpu.VMEM((REF_ROWS, HALF), F32)],
    )
    got = gather_slots(stat, False)

    wide = ((nblocks, REF_ROWS, LANES), F32, "block")
    far_expo, own_expo = call("spread", spread_kernel, nblocks, [(expo, "block")], [wide, wide], [])

    def back(name, expo, more):
        half = ((REF_ROWS, HALF), F32, "all")
        return call(
            name,
            lambda *a: back_kernel(nblocks, *a),
            nblocks,
            [(me, "scalar")] + [(g, "all") for g in got] + [(stat, "block"), (expo, "block")] + [(x, "block") for x in images],
            [half, half] + more,
            [pltpu.VMEM((2 * REF_ROWS, LANES), BF16), pltpu.VMEM((REF_ROWS, LANES), F32)],
            4,
        )

    far_keep, far_send, logs = back("far_sums", far_expo, [((8, HALF), F32, "all")])
    far_got = swap(far_send, "dom", 1)
    keep, send = back("own_sums", own_expo, [])
    own_got = swap(send, "dom", 1)
    far_sum = swap((far_keep + far_got).astype(BF16), "cls", 1)
    (sums,) = call(
        "flat_rows",
        flat_kernel,
        1,
        [(keep, "all"), (own_got, "all"), (far_sum, "all")],
        [((CLS, GROUP * 8), F32, "all")],
        [
            pltpu.VMEM((HALF * CLS, HALF), F32),
            pltpu.VMEM((CLS, HALF, HALF), F32),
            pltpu.VMEM((GROUP // HALF, CLS * 8, HALF), F32),
        ],
    )
    return sums, logs[0, :PER_DEV]


def solution(mesh):
    placed = (
        P(("groups", "cls", "dom"), None),
        P(("groups", "cls"), None),
        P(("groups", "cls", "dom"), None),
        P(("groups", "cls", "dom"), None, None),
        P(),
    )
    return jax.shard_map(
        per_device,
        mesh=mesh,
        in_specs=placed,
        out_specs=(P(("groups", "cls"), "dom"), P(("groups", "cls", "dom"))),
        check_vma=False,
    )
```

```python
import math

import jax
import jax.numpy as jnp
import numpy as np
from jax import lax
from jax.experimental import pallas as pl
from jax.experimental.pallas import tpu as pltpu
from jax.sharding import PartitionSpec as P

ROT = 72
CYCLES = 64
CLASS_LIST_SIZE = 32
BOX = 256
TRANS = 3
PER_DEV = 4
CLS = 8
SLOTS = 4
LANES = 256
HALF = 128
GROUP = 16 * ROT
ROWS = ROT * PER_DEV
REF_ROWS = ROT * CLS
STEPS = ROT // 4
HALF_TURN = ROWS // 2
CODED = 3 * 16
LOWEST = -1e30
VMEM = 20 * 1024 * 1024

F32 = jnp.float32
BF16 = jnp.bfloat16


def frequency_rows():
    row = lax.broadcasted_iota(jnp.int32, (HALF_TURN, HALF), 0)
    lane = lax.broadcasted_iota(jnp.int32, (HALF_TURN, HALF), 1)
    line = (lane % 8) * 16 + lane // 8
    radius = (line // 2 + 1).astype(F32) * (1.0 / BOX)
    angle = (2 * (row // PER_DEV) + line % 2).astype(F32) * (0.5 / ROT)
    c, s = cos_sin_turns(angle)
    return radius * c, radius * s


def half_turn_polynomials():
    t = np.cos(np.pi * (np.arange(400) + 0.5) / 400)
    z = (t + 1) / 8
    v = np.sqrt(z)
    sin_fit = np.polynomial.chebyshev.Chebyshev.fit(z, np.sin(np.pi * v) / v, 4, domain=[0, 0.25])
    cos_fit = np.polynomial.chebyshev.Chebyshev.fit(z, np.cos(np.pi * v), 5, domain=[0, 0.25])
    to_list = lambda f: [float(c) for c in f.convert(kind=np.polynomial.Polynomial).coef]
    return to_list(sin_fit), to_list(cos_fit)


SIN_COEF, COS_COEF = half_turn_polynomials()


def horner(coef, z):
    total = jnp.full_like(z, coef[-1])
    for c in coef[-2::-1]:
        total = total * z + c
    return total


def cos_sin_turns(u):
    v = u - jnp.round(u)
    z = v * v
    s = v * horner(SIN_COEF, z)
    c = horner(COS_COEF, z)
    s2 = s + s
    return 1.0 - s2 * s, s2 * c


def turn_major(x_ref, grid_ref, lines_ref, out_ref, count):
    for g in range(16):
        for tile in range(GROUP // HALF):
            start = g * GROUP + tile * HALF
            grid_ref[tile, pl.ds(g, count, stride=16), :] = x_ref[:, start : start + HALF].astype(F32)
    for h in range(16):
        tile, shift = divmod(ROT * h, HALF)
        if shift + ROT <= HALF:
            part = grid_ref[tile]
            if shift:
                part = pltpu.roll(part, HALF - shift, 1)
        else:
            part = jnp.concatenate([grid_ref[tile], grid_ref[tile + 1]], axis=1)
            part = pltpu.roll(part, LANES - shift, 1)[:, :HALF]
        lines_ref[:, :, h] = part.reshape(count, 2, 8, HALF)
    for p in range(count):
        for half in range(2):
            turns = lines_ref[p, half].reshape(HALF, HALF).T
            out_ref[half, pl.ds(p, ROT, stride=count), :] = turns[:ROT]


def particle_kernel(
    nbit, x_any, list_any, move_any, out_ref, x_ref, list_ref, move_ref, grid_ref, lines_ref, turns_ref, sems
):
    pairs = ((x_any, x_ref), (list_any, list_ref), (move_any, move_ref))
    copies = [pltpu.make_async_copy(a, b, sems.at[n]) for n, (a, b) in enumerate(pairs)]
    for copy in copies:
        copy.start()
    copies[0].wait()
    turn_major(x_ref, grid_ref, lines_ref, turns_ref, PER_DEV)
    out_ref[:ROWS] = jnp.concatenate([turns_ref[0], turns_ref[1]], axis=1).astype(BF16)
    copies[1].wait()
    copies[2].wait()
    lists = list_ref[...]
    lane = lax.broadcasted_iota(jnp.int32, (PER_DEV, LANES), 1)
    parts = []
    for b in range(nbit):
        named = jnp.zeros((PER_DEV, LANES), F32)
        for j in range(CLASS_LIST_SIZE):
            named = jnp.where(lists[:, j : j + 1] == lane + b * LANES, 1.0, named)
        parts += [named, named]
    row = lax.broadcasted_iota(jnp.int32, (8, LANES), 0) % PER_DEV
    lane = lax.broadcasted_iota(jnp.int32, (8, LANES), 1)
    moves = jnp.zeros((8, LANES), F32)
    for p in range(PER_DEV):
        for t in range(TRANS):
            for a in range(2):
                here = (row == p) & (lane == 8 * a + t)
                moves = jnp.where(here, move_ref[t, a, p].astype(F32), moves)
    parts.append(moves)
    if nbit % 2 == 0:
        parts.append(jnp.zeros((8, LANES), F32))
    out_ref[ROWS:] = jnp.concatenate(parts, axis=0).astype(BF16)


def reference_kernel(x_ref, w_ref, out_ref, *rest):
    freq_refs, (grid_ref, lines_ref, turns_ref) = rest[:-3], rest[-3:]
    turn_major(x_ref, grid_ref, lines_ref, turns_ref, CLS)
    scaled = (jnp.concatenate([turns_ref[0], turns_ref[1]], axis=1) * w_ref[...]).astype(BF16)
    out_ref[:REF_ROWS] = scaled
    out_ref[REF_ROWS:] = scaled
    for ref, f in zip(freq_refs, frequency_rows()):
        ref[...] = f


def shift_kernel(nbit, block_ref, fx_ref, fy_ref, x_ref, bits_ref):
    first = ROWS + 16 * (nbit // 2)
    m = block_ref[0, first : first + 16].astype(F32)[8 * (nbit % 2) : 8 * (nbit % 2) + 8]
    m = jnp.concatenate([m, m], axis=0)
    moves = [
        (jnp.broadcast_to(m[:, t : t + 1], (16, HALF)), jnp.broadcast_to(m[:, 8 + t : 9 + t], (16, HALF)))
        for t in range(TRANS)
    ]
    bits_ref[0] = block_ref[0, ROWS : ROWS + bits_ref.shape[1]]

    def step(q, carry):
        rows = pl.ds(pl.multiple_of(q * 16, 16), 16)
        later = pl.ds(pl.multiple_of(q * 16, 16) + HALF_TURN, 16)
        fx = fx_ref[rows, :]
        fy = fy_ref[rows, :]
        near = block_ref[0, rows, :].astype(F32)
        far = block_ref[0, later, :].astype(F32)
        for t in range(TRANS):
            dx, dy = moves[t]
            c, s = cos_sin_turns(fx * dx + fy * dy)
            a, b = near[:, :HALF], near[:, HALF:]
            x_ref[0, q, t * 16 : t * 16 + 16, :HALF] = (a * c + b * s).astype(BF16)
            x_ref[0, q, t * 16 : t * 16 + 16, HALF:] = (b * c - a * s).astype(BF16)
            a, b = far[:, :HALF], far[:, HALF:]
            x_ref[0, q + STEPS // 2, t * 16 : t * 16 + 16, :HALF] = (a * c - b * s).astype(BF16)
            x_ref[0, q + STEPS // 2, t * 16 : t * 16 + 16, HALF:] = (b * c + a * s).astype(BF16)
        return carry

    lax.fori_loop(0, STEPS // 2, step, 0, unroll=3)


def xor_lanes(x, step):
    lane = lax.broadcasted_iota(jnp.int32, x.shape, x.ndim - 1)
    width = x.shape[-1]
    down = pltpu.roll(x, width - step, x.ndim - 1)
    up = pltpu.roll(x, step, x.ndim - 1)
    return jnp.where((lane // step) % 2 == 0, down, up)


def xor_slots(x, bits):
    if bits & 1:
        x = xor_lanes(x, 64)
    if bits & 2:
        x = xor_lanes(x, 4)
    return x


def live_lanes(shape):
    lane = lax.broadcasted_iota(jnp.int32, shape, 1)
    return (lane % 64 < 16 * TRANS) & (lane % 16 < 8)


def images_of(x_refs, q):
    empty = jnp.zeros((16, LANES), BF16)
    return jnp.concatenate([v for x in x_refs for v in (x[0, q], empty)], axis=0)


def score_kernel(nbit, *refs):
    x_refs = refs[:SLOTS]
    bit_refs = refs[SLOTS : 2 * SLOTS]
    own_ref, far_ref, e_ref, stat_ref, acc_ref, pair_ref = refs[2 * SLOTS :]

    src = lax.broadcasted_iota(jnp.int32, (SLOTS * 16, HALF), 0)
    dst = lax.broadcasted_iota(jnp.int32, (SLOTS * 16, HALF), 1)
    slot = dst // 64 + 2 * (dst % 16 // 4)
    place = ((src == slot * 16 + dst % 4) & live_lanes(src.shape)).astype(F32).astype(BF16)
    lane = lax.broadcasted_iota(jnp.int32, (2 * CLS, LANES), 1)
    row = lax.broadcasted_iota(jnp.int32, (2 * CLS, LANES), 0)
    wanted = (lax.axis_index("cls") ^ row // CLS) * CLS + row % CLS
    named = jnp.zeros((2 * CLS, SLOTS * 16), F32)
    for b in range(nbit):
        pick = (lane + b * LANES == wanted).astype(F32).astype(BF16)
        first = 16 * (b // 2)
        bits = jnp.concatenate([r[0, first : first + 16] for r in bit_refs], axis=0)
        if b % 2:
            bits = jnp.concatenate(
                [v for s in range(SLOTS) for v in (bits[s * 16 + 8 : s * 16 + 16], bits[s * 16 : s * 16 + 8])],
                axis=0,
            )
        named += lax.dot_general(pick, bits, (((1,), (1,)), ((), ())), preferred_element_type=F32)
    masks = jnp.dot(named.astype(BF16), place, preferred_element_type=F32)
    turn = lax.broadcasted_iota(jnp.int32, (CLS, HALF), 1) % 16 // 4
    images = jnp.concatenate([images_of(x_refs, q) for q in range(STEPS)], axis=1)
    for side, ref in enumerate((own_ref, far_ref)):
        turned = jnp.concatenate([ref[q * 32 : q * 32 + REF_ROWS] for q in range(STEPS)], axis=1)
        acc_ref[side] = lax.dot_general(turned, images, (((1,), (1,)), ((), ())), preferred_element_type=F32)
    stats = []
    for side in range(2):
        mask = masks[side * CLS : side * CLS + CLS] > 0.5

        def at(i, side=side):
            i = i % ROT
            return acc_ref[side, i * 8 : i * 8 + 8, :HALF], acc_ref[side, i * 8 : i * 8 + 8, HALF:]

        for i in range(ROT):
            (a, b), (c, d) = at(i), at(i + 1)
            low = a + pltpu.roll(c, HALF - 4, 1)
            high = b + pltpu.roll(d, HALF - 4, 1)
            pair_ref[side, i * 8 : i * 8 + 8] = jnp.where(turn % 2 == 0, low, pltpu.roll(high, 4, 1))
        tops = [jnp.full((CLS, HALF), LOWEST, F32)] * 4
        for i in range(ROT):
            n = (i + 2) % ROT
            s = pair_ref[side, i * 8 : i * 8 + 8] + pltpu.roll(pair_ref[side, n * 8 : n * 8 + 8], HALF - 8, 1)
            s = jnp.where(mask, s, LOWEST)
            e_ref[0, side, i * 8 : i * 8 + 8] = s
            tops[i % 4] = jnp.maximum(tops[i % 4], s)
        top = jnp.maximum(jnp.maximum(tops[0], tops[1]), jnp.maximum(tops[2], tops[3]))
        top = jnp.broadcast_to(jnp.max(top, axis=0, keepdims=True), (CLS, HALF))
        top = jnp.maximum(top, xor_lanes(top, 16))
        top = jnp.maximum(top, xor_lanes(top, 32))
        base = jnp.where(top == LOWEST, 0.0, top)
        totals = [jnp.zeros((CLS, HALF), F32)] * 4
        for i in range(ROT):
            e = jnp.exp(e_ref[0, side, i * 8 : i * 8 + 8] - base)
            e_ref[0, side, i * 8 : i * 8 + 8] = e
            totals[i % 4] += e
        total = (totals[0] + totals[1]) + (totals[2] + totals[3])
        total = jnp.broadcast_to(jnp.sum(total, axis=0, keepdims=True), (CLS, HALF))
        total = total + xor_lanes(total, 16)
        total = total + xor_lanes(total, 32)
        stats += [top, total]
    out = stats[3]
    line = lax.broadcasted_iota(jnp.int32, (CLS, HALF), 0)
    for r in (2, 1, 0):
        out = jnp.where(line == r, stats[r], out)
    stat_ref[0] = out


def factors(side, got_refs, stat_ref, nblocks, n):
    stats = [
        xor_slots(got_refs[low][high, n ^ high], low) for high in range(nblocks) for low in range(SLOTS)
    ]
    spread = lambda x, r: jnp.broadcast_to(x[r : r + 1], (8, HALF))
    pairs = [(spread(x, r), spread(x, r + 1)) for x in stats for r in (0, 2)]
    best = pairs[0][0]
    for top, _ in pairs[1:]:
        best = jnp.maximum(best, top)
    evidence = jnp.zeros((8, HALF), F32)
    for top, total in pairs:
        evidence = evidence + total * jnp.exp(top - best)
    factor = jnp.where(live_lanes((8, HALF)), jnp.exp(spread(stat_ref[0], 2 * side) - best) / evidence, 0.0)
    return factor, best + jnp.log(evidence)


def spread_kernel(e_ref, far_ref, own_ref):
    turn = lax.broadcasted_iota(jnp.int32, (8, HALF), 1) % 16 // 4
    for side, out_ref in enumerate((own_ref, far_ref)):

        def weights(i):
            i = i % ROT
            w = e_ref[0, side, i * 8 : i * 8 + 8]
            return jnp.where(turn == 0, w, 0.0), jnp.where(turn == 1, w, 0.0)

        def two_turns(now, before):
            return now[0] + pltpu.roll(before[0], 4, 1), pltpu.roll(now[1], HALF - 4, 1) + before[1]

        plain = [weights(i) for i in (-3, -2, -1)]
        pairs = [two_turns(plain[1], plain[0]), two_turns(plain[2], plain[1])]
        before = plain[2]
        for i in range(ROT):
            now = weights(i)
            pairs.append(two_turns(now, before))
            before = now
            last = pairs.pop(0)
            (a, b), (c, d) = pairs[-1], last
            out_ref[0, i * 8 : i * 8 + 8, :HALF] = a + pltpu.roll(c, 8, 1)
            out_ref[0, i * 8 : i * 8 + 8, HALF:] = b + pltpu.roll(d, 8, 1)


def back_kernel(side, nblocks, *refs):
    got_refs = [refs[k] for k in (0, 1, 3, 2)]
    stat_ref, e_ref = refs[SLOTS : SLOTS + 2]
    x_refs = refs[SLOTS + 2 : 2 * SLOTS + 2]
    keep_ref, send_ref, *log_ref = refs[2 * SLOTS + 2 : -2]
    w_ref, acc_ref = refs[-2:]
    n = pl.program_id(0) if nblocks > 1 else 0
    factor, logs = factors(side, got_refs, stat_ref, nblocks, n)
    if log_ref:

        @pl.when(n == 0)
        def _():
            log_ref[0][...] = logs

    turn = lax.broadcasted_iota(jnp.int32, (8, HALF), 1) % 16 // 4
    low = jnp.where(turn == 0, factor, 0.0)
    high = pltpu.roll(jnp.where(turn == 1, factor, 0.0), HALF - 4, 1)
    low, high = (f + pltpu.roll(f, 4, 1) for f in (low, high))
    low, high = (f + pltpu.roll(f, 8, 1) for f in (low, high))
    both = jnp.concatenate([low, high], axis=1)
    both = jnp.concatenate([both, both], axis=0)
    for i in range(0, REF_ROWS, 16):
        pair = (e_ref[0, i : i + 16] * both).astype(BF16)
        w_ref[i : i + 16] = pair
        w_ref[REF_ROWS + i : REF_ROWS + i + 16] = pair

    turned = jnp.concatenate(
        [w_ref[(STEPS - q) * 32 : (STEPS - q) * 32 + REF_ROWS] for q in range(STEPS)], axis=1
    )
    images = jnp.concatenate([images_of(x_refs, q) for q in range(STEPS)], axis=0)
    made = jnp.dot(turned, images, preferred_element_type=F32)
    if nblocks > 1:
        acc_ref[...] = jnp.where(n == 0, made, acc_ref[...] + made)
        made = acc_ref[...]
    first = lax.axis_index("dom") == 0
    keep_ref[...] = jnp.where(first, made[:, :HALF], made[:, HALF:])
    send_ref[...] = jnp.where(first, made[:, HALF:], made[:, :HALF])


def flat_kernel(a_ref, b_ref, c_ref, out_ref, sum_ref, lines_ref, grid_ref):
    sum_ref[:REF_ROWS] = a_ref[...] + b_ref[...] + c_ref[...].astype(F32)
    lane = lax.broadcasted_iota(jnp.int32, (CLS * 8, HALF), 1)
    for c in range(CLS):
        turns = sum_ref[pl.ds(c, HALF, stride=CLS), :]
        lines_ref[c] = turns.T
    for tile in range(GROUP // HALF):
        made = None
        for h in range(16):
            start = ROT * h - tile * HALF
            if start >= HALF or start + ROT <= 0:
                continue
            part = lines_ref[:, h * 8 : h * 8 + 8, :].reshape(CLS * 8, HALF)
            if start % HALF:
                part = pltpu.roll(part, start % HALF, 1)
            made = part if made is None else jnp.where(lane >= start, part, made)
        grid_ref[tile] = made
        for g in range(8):
            start = g * GROUP + tile * HALF
            out_ref[:, start : start + HALF] = grid_ref[tile, pl.ds(g, CLS, stride=8), :]


def swap(x, axis, bits):
    return lax.ppermute(x, axis, [(i, i ^ bits) for i in range(lax.axis_size(axis))])


def gather_slots(block, relay):
    if lax.axis_size("cls") == 2 * SLOTS:
        if relay:
            r2 = swap(block, "cls", 4)
            r1 = swap(block, "cls", 2)
            r3 = swap(r2, "cls", 2)
        else:
            r1, r2, r3 = (swap(block, "cls", bits) for bits in (2, 4, 6))
        return [x[None] for x in (block, r1, r2, r3)]
    slots = block[None]
    bits = 2
    while bits < lax.axis_size("cls"):
        slots = jnp.concatenate([slots, swap(slots, "cls", bits)], axis=0)
        bits *= 2
    return [slots[s::SLOTS] for s in range(SLOTS)]


def call(name, body, nblocks, inputs, outputs, scratch, micros=1, vmem=VMEM):
    def spec(shape, kind):
        if kind == "any":
            return pl.BlockSpec(memory_space=pltpu.HBM)
        if nblocks == 1:
            return pl.BlockSpec(memory_space=pltpu.VMEM)
        rest = (0,) * (len(shape) - 1)
        if kind == "block":
            return pl.BlockSpec((1,) + shape[1:], lambda n: (n,) + rest)
        return pl.BlockSpec(shape, lambda n: (0,) + rest)

    grid = {"grid": (nblocks,)} if nblocks > 1 else {}
    return pl.pallas_call(
        body,
        out_shape=tuple(jax.ShapeDtypeStruct(shape, dtype) for shape, dtype, _ in outputs),
        in_specs=[spec(x.shape, kind) for x, kind in inputs],
        out_specs=tuple(spec(shape, kind) for shape, _, kind in outputs),
        scratch_shapes=scratch,
        compiler_params=pltpu.CompilerParams(vmem_limit_bytes=vmem),
        cost_estimate=pl.CostEstimate(flops=micros * 10**9, bytes_accessed=micros * 10**6, transcendentals=0),
        name=name,
        **grid,
    )(*[x for x, _ in inputs])


def per_device(particles, references, class_lists, offsets, inv_noise):
    holders = lax.axis_size("cls")
    nblocks = holders // 2 // SLOTS
    nbit = -(-holders * CLS // LANES)
    extra = -(-(8 * nbit + 8) // 16) * 16
    rows = ROWS + extra

    def scratch(count):
        return [
            pltpu.VMEM((GROUP // HALF, count * 16, HALF), F32),
            pltpu.VMEM((count, 2, 16, 8, HALF), F32),
            pltpu.VMEM((2, ROT * count, HALF), F32),
        ]

    moves = jnp.transpose(offsets, (1, 2, 0))
    (block,) = call(
        "particle_turns",
        lambda *a: particle_kernel(nbit, *a),
        1,
        [(particles, "any"), (class_lists, "any"), (moves, "any")],
        [((rows, LANES), BF16, "all")],
        [
            pltpu.VMEM(particles.shape, BF16),
            pltpu.VMEM(class_lists.shape, jnp.int32),
            pltpu.SMEM(moves.shape, jnp.int32),
        ]
        + scratch(PER_DEV)
        + [pltpu.SemaphoreType.DMA((3,))],
        vmem=60 * 1024 * 1024,
    )
    slots = gather_slots(block, True)
    far_references = swap(references, "cls", 1)

    weights = jnp.repeat(inv_noise.reshape(8, 8).T, 2, axis=0).reshape(1, HALF)
    weights = jnp.concatenate([weights, weights], axis=1)
    turned = ((2 * REF_ROWS, LANES), BF16, "all")
    freq = ((HALF_TURN, HALF), F32, "all")
    own_refs, fx, fy = call(
        "own_references", reference_kernel, 1, [(references, "all"), (weights, "all")], [turned, freq, freq], scratch(CLS)
    )
    (far_refs,) = call(
        "far_references", reference_kernel, 1, [(far_references, "all"), (weights, "all")], [turned], scratch(CLS)
    )

    bit_rows = 16 * -(-nbit // 2)
    images, bits = [], []
    for s, slot in enumerate(slots):
        if s == SLOTS - 1:
            fx, far_refs = lax.optimization_barrier((fx, far_refs))
        x, b = call(
            "shifted",
            lambda *a: shift_kernel(nbit, *a),
            nblocks,
            [(slot, "block"), (fx, "all"), (fy, "all")],
            [((nblocks, STEPS, CODED, LANES), BF16, "block"), ((nblocks, bit_rows, LANES), BF16, "block")],
            [],
        )
        images.append(x)
        bits.append(b)

    expo, stat = call(
        "scores",
        lambda *a: score_kernel(nbit, *a),
        nblocks,
        [(x, "block") for x in images + bits] + [(own_refs, "all"), (far_refs, "all")],
        [((nblocks, 2, REF_ROWS, HALF), F32, "block"), ((nblocks, 8, HALF), F32, "block")],
        [pltpu.VMEM((2, REF_ROWS, LANES), F32), pltpu.VMEM((2, REF_ROWS, HALF), F32)],
    )
    got = gather_slots(stat, False)

    wide = ((nblocks, REF_ROWS, LANES), F32, "block")
    far_expo, own_expo = call("spread", spread_kernel, nblocks, [(expo, "block")], [wide, wide], [])

    def back(name, side, expo, more):
        half = ((REF_ROWS, HALF), F32, "all")
        return call(
            name,
            lambda *a: back_kernel(side, nblocks, *a),
            nblocks,
            [(g, "all") for g in [got[k] for k in (0, 1, 3, 2)]] + [(stat, "block"), (expo, "block")] + [(x, "block") for x in images],
            [half, half] + more,
            [pltpu.VMEM((2 * REF_ROWS, LANES), BF16), pltpu.VMEM((REF_ROWS, LANES), F32)],
            4,
        )

    far_keep, far_send = back("far_sums", 1, far_expo, [])
    far_got = swap(far_send, "dom", 1)
    keep, send, logs = back("own_sums", 0, own_expo, [((8, HALF), F32, "all")])
    own_got = swap(send, "dom", 1)
    far_sum = swap((far_keep + far_got).astype(BF16), "cls", 1)
    (sums,) = call(
        "flat_rows",
        flat_kernel,
        1,
        [(keep, "all"), (own_got, "all"), (far_sum, "all")],
        [((CLS, GROUP * 8), F32, "all")],
        [
            pltpu.VMEM((HALF * CLS, HALF), F32),
            pltpu.VMEM((CLS, HALF, HALF), F32),
            pltpu.VMEM((GROUP // HALF, CLS * 8, HALF), F32),
        ],
    )
    return sums, logs[0, :PER_DEV]


def solution(mesh):
    placed = (
        P(("groups", "cls", "dom"), None),
        P(("groups", "cls"), None),
        P(("groups", "cls", "dom"), None),
        P(("groups", "cls", "dom"), None, None),
        P(),
    )
    return jax.shard_map(
        per_device,
        mesh=mesh,
        in_specs=placed,
        out_specs=(P(("groups", "cls"), "dom"), P(("groups", "cls", "dom"))),
        check_vma=False,
    )
```

```python
import math

import jax
import jax.numpy as jnp
import numpy as np
from jax import lax
from jax.experimental import pallas as pl
from jax.experimental.pallas import tpu as pltpu
from jax.sharding import PartitionSpec as P

ROT = 72
CYCLES = 64
CLASS_LIST_SIZE = 32
BOX = 256
TRANS = 3
PER_DEV = 4
CLS = 8
SLOTS = 4
LANES = 256
HALF = 128
GROUP = 16 * ROT
ROWS = ROT * PER_DEV
REF_ROWS = ROT * CLS
STEPS = ROT // 4
HALF_TURN = ROWS // 2
CODED = 3 * 16
LOWEST = -1e30
VMEM = 20 * 1024 * 1024

F32 = jnp.float32
BF16 = jnp.bfloat16


def frequency_rows():
    row = lax.broadcasted_iota(jnp.int32, (HALF_TURN, HALF), 0)
    lane = lax.broadcasted_iota(jnp.int32, (HALF_TURN, HALF), 1)
    line = (lane % 8) * 16 + lane // 8
    radius = (line // 2 + 1).astype(F32) * (1.0 / BOX)
    angle = (2 * (row // PER_DEV) + line % 2).astype(F32) * (0.5 / ROT)
    c, s = cos_sin_turns(angle)
    return radius * c, radius * s


def half_turn_polynomials():
    t = np.cos(np.pi * (np.arange(400) + 0.5) / 400)
    z = (t + 1) / 8
    v = np.sqrt(z)
    sin_fit = np.polynomial.chebyshev.Chebyshev.fit(z, np.sin(np.pi * v) / v, 4, domain=[0, 0.25])
    cos_fit = np.polynomial.chebyshev.Chebyshev.fit(z, np.cos(np.pi * v), 5, domain=[0, 0.25])
    to_list = lambda f: [float(c) for c in f.convert(kind=np.polynomial.Polynomial).coef]
    return to_list(sin_fit), to_list(cos_fit)


SIN_COEF, COS_COEF = half_turn_polynomials()


def horner(coef, z):
    total = jnp.full_like(z, coef[-1])
    for c in coef[-2::-1]:
        total = total * z + c
    return total


def cos_sin_turns(u):
    v = u - jnp.round(u)
    z = v * v
    s = v * horner(SIN_COEF, z)
    c = horner(COS_COEF, z)
    s2 = s + s
    return 1.0 - s2 * s, s2 * c


def turn_major(x_ref, grid_ref, lines_ref, out_ref, count):
    for g in range(16):
        for tile in range(GROUP // HALF):
            start = g * GROUP + tile * HALF
            grid_ref[tile, pl.ds(g, count, stride=16), :] = x_ref[:, start : start + HALF].astype(F32)
    for h in range(16):
        tile, shift = divmod(ROT * h, HALF)
        if shift + ROT <= HALF:
            part = grid_ref[tile]
            if shift:
                part = pltpu.roll(part, HALF - shift, 1)
        else:
            part = jnp.concatenate([grid_ref[tile], grid_ref[tile + 1]], axis=1)
            part = pltpu.roll(part, LANES - shift, 1)[:, :HALF]
        lines_ref[:, :, h] = part.reshape(count, 2, 8, HALF)
    for p in range(count):
        for half in range(2):
            turns = lines_ref[p, half].reshape(HALF, HALF).T
            out_ref[half, pl.ds(p, ROT, stride=count), :] = turns[:ROT]


def particle_kernel(
    nbit, x_any, list_any, move_any, out_ref, x_ref, list_ref, move_ref, grid_ref, lines_ref, turns_ref, sems
):
    pairs = ((x_any, x_ref), (list_any, list_ref), (move_any, move_ref))
    copies = [pltpu.make_async_copy(a, b, sems.at[n]) for n, (a, b) in enumerate(pairs)]
    for copy in copies:
        copy.start()
    copies[0].wait()
    turn_major(x_ref, grid_ref, lines_ref, turns_ref, PER_DEV)
    out_ref[:ROWS] = jnp.concatenate([turns_ref[0], turns_ref[1]], axis=1).astype(BF16)
    copies[1].wait()
    copies[2].wait()
    lists = list_ref[...]
    lane = lax.broadcasted_iota(jnp.int32, (PER_DEV, LANES), 1)
    parts = []
    for b in range(nbit):
        named = jnp.zeros((PER_DEV, LANES), F32)
        for j in range(CLASS_LIST_SIZE):
            named = jnp.where(lists[:, j : j + 1] == lane + b * LANES, 1.0, named)
        parts += [named, named]
    row = lax.broadcasted_iota(jnp.int32, (8, LANES), 0) % PER_DEV
    lane = lax.broadcasted_iota(jnp.int32, (8, LANES), 1)
    moves = jnp.zeros((8, LANES), F32)
    for p in range(PER_DEV):
        for t in range(TRANS):
            for a in range(2):
                here = (row == p) & (lane == 8 * a + t)
                moves = jnp.where(here, move_ref[t, a, p].astype(F32), moves)
    parts.append(moves)
    if nbit % 2 == 0:
        parts.append(jnp.zeros((8, LANES), F32))
    out_ref[ROWS:] = jnp.concatenate(parts, axis=0).astype(BF16)


def reference_kernel(x_ref, w_ref, out_ref, *rest):
    freq_refs, (grid_ref, lines_ref, turns_ref) = rest[:-3], rest[-3:]
    turn_major(x_ref, grid_ref, lines_ref, turns_ref, CLS)
    scaled = (jnp.concatenate([turns_ref[0], turns_ref[1]], axis=1) * w_ref[...]).astype(BF16)
    out_ref[:REF_ROWS] = scaled
    out_ref[REF_ROWS:] = scaled
    for ref, f in zip(freq_refs, frequency_rows()):
        ref[...] = f


def shift_kernel(nbit, block_ref, fx_ref, fy_ref, x_ref, bits_ref):
    first = ROWS + 16 * (nbit // 2)
    m = block_ref[0, first : first + 16].astype(F32)[8 * (nbit % 2) : 8 * (nbit % 2) + 8]
    m = jnp.concatenate([m, m], axis=0)
    moves = [
        (jnp.broadcast_to(m[:, t : t + 1], (16, HALF)), jnp.broadcast_to(m[:, 8 + t : 9 + t], (16, HALF)))
        for t in range(TRANS)
    ]
    bits_ref[0] = block_ref[0, ROWS : ROWS + bits_ref.shape[1]]

    def step(q, carry):
        rows = pl.ds(pl.multiple_of(q * 16, 16), 16)
        later = pl.ds(pl.multiple_of(q * 16, 16) + HALF_TURN, 16)
        fx = fx_ref[rows, :]
        fy = fy_ref[rows, :]
        near = block_ref[0, rows, :].astype(F32)
        far = block_ref[0, later, :].astype(F32)
        for t in range(TRANS):
            dx, dy = moves[t]
            c, s = cos_sin_turns(fx * dx + fy * dy)
            a, b = near[:, :HALF], near[:, HALF:]
            x_ref[0, q, t * 16 : t * 16 + 16, :HALF] = (a * c + b * s).astype(BF16)
            x_ref[0, q, t * 16 : t * 16 + 16, HALF:] = (b * c - a * s).astype(BF16)
            a, b = far[:, :HALF], far[:, HALF:]
            x_ref[0, q + STEPS // 2, t * 16 : t * 16 + 16, :HALF] = (a * c - b * s).astype(BF16)
            x_ref[0, q + STEPS // 2, t * 16 : t * 16 + 16, HALF:] = (b * c + a * s).astype(BF16)
        return carry

    lax.fori_loop(0, STEPS // 2, step, 0, unroll=9)


def xor_lanes(x, step):
    lane = lax.broadcasted_iota(jnp.int32, x.shape, x.ndim - 1)
    width = x.shape[-1]
    down = pltpu.roll(x, width - step, x.ndim - 1)
    up = pltpu.roll(x, step, x.ndim - 1)
    return jnp.where((lane // step) % 2 == 0, down, up)


def xor_slots(x, bits):
    if bits & 1:
        x = xor_lanes(x, 64)
    if bits & 2:
        x = xor_lanes(x, 4)
    return x


def live_lanes(shape):
    lane = lax.broadcasted_iota(jnp.int32, shape, 1)
    return (lane % 64 < 16 * TRANS) & (lane % 16 < 8)


def images_of(x_refs, q):
    empty = jnp.zeros((16, LANES), BF16)
    return jnp.concatenate([v for x in x_refs for v in (x[0, q], empty)], axis=0)


def score_kernel(nbit, *refs):
    early = SLOTS - 1
    block_ref, fx_ref, fy_ref, own_ref, far_ref, x_ref, e_ref, stat_ref, bits_ref, acc_ref, pair_ref = refs[2 * early :]
    x_refs = refs[:early] + (x_ref,)
    bit_refs = refs[early : 2 * early] + (bits_ref,)
    shift_kernel(nbit, block_ref, fx_ref, fy_ref, x_ref, bits_ref)

    src = lax.broadcasted_iota(jnp.int32, (SLOTS * 16, HALF), 0)
    dst = lax.broadcasted_iota(jnp.int32, (SLOTS * 16, HALF), 1)
    slot = dst // 64 + 2 * (dst % 16 // 4)
    place = ((src == slot * 16 + dst % 4) & live_lanes(src.shape)).astype(F32).astype(BF16)
    lane = lax.broadcasted_iota(jnp.int32, (2 * CLS, LANES), 1)
    row = lax.broadcasted_iota(jnp.int32, (2 * CLS, LANES), 0)
    wanted = (lax.axis_index("cls") ^ row // CLS) * CLS + row % CLS
    named = jnp.zeros((2 * CLS, SLOTS * 16), F32)
    for b in range(nbit):
        pick = (lane + b * LANES == wanted).astype(F32).astype(BF16)
        first = 16 * (b // 2)
        bits = jnp.concatenate([r[0, first : first + 16] for r in bit_refs], axis=0)
        if b % 2:
            bits = jnp.concatenate(
                [v for s in range(SLOTS) for v in (bits[s * 16 + 8 : s * 16 + 16], bits[s * 16 : s * 16 + 8])],
                axis=0,
            )
        named += lax.dot_general(pick, bits, (((1,), (1,)), ((), ())), preferred_element_type=F32)
    masks = jnp.dot(named.astype(BF16), place, preferred_element_type=F32)
    turn = lax.broadcasted_iota(jnp.int32, (CLS, HALF), 1) % 16 // 4
    images = jnp.concatenate([images_of(x_refs, q) for q in range(STEPS)], axis=1)
    for side, ref in enumerate((own_ref, far_ref)):
        turned = jnp.concatenate([ref[q * 32 : q * 32 + REF_ROWS] for q in range(STEPS)], axis=1)
        acc_ref[side] = lax.dot_general(turned, images, (((1,), (1,)), ((), ())), preferred_element_type=F32)
    stats = []
    for side in range(2):
        mask = masks[side * CLS : side * CLS + CLS] > 0.5

        def at(i, side=side):
            i = i % ROT
            return acc_ref[side, i * 8 : i * 8 + 8, :HALF], acc_ref[side, i * 8 : i * 8 + 8, HALF:]

        for i in range(ROT):
            (a, b), (c, d) = at(i), at(i + 1)
            low = a + pltpu.roll(c, HALF - 4, 1)
            high = b + pltpu.roll(d, HALF - 4, 1)
            pair_ref[side, i * 8 : i * 8 + 8] = jnp.where(turn % 2 == 0, low, pltpu.roll(high, 4, 1))
        tops = [jnp.full((CLS, HALF), LOWEST, F32)] * 4
        for i in range(ROT):
            n = (i + 2) % ROT
            s = pair_ref[side, i * 8 : i * 8 + 8] + pltpu.roll(pair_ref[side, n * 8 : n * 8 + 8], HALF - 8, 1)
            s = jnp.where(mask, s, LOWEST)
            e_ref[0, side, i * 8 : i * 8 + 8] = s
            tops[i % 4] = jnp.maximum(tops[i % 4], s)
        top = jnp.maximum(jnp.maximum(tops[0], tops[1]), jnp.maximum(tops[2], tops[3]))
        top = jnp.broadcast_to(jnp.max(top, axis=0, keepdims=True), (CLS, HALF))
        top = jnp.maximum(top, xor_lanes(top, 16))
        top = jnp.maximum(top, xor_lanes(top, 32))
        base = jnp.where(top == LOWEST, 0.0, top)
        totals = [jnp.zeros((CLS, HALF), F32)] * 4
        for i in range(ROT):
            e = jnp.exp(e_ref[0, side, i * 8 : i * 8 + 8] - base)
            e_ref[0, side, i * 8 : i * 8 + 8] = e
            totals[i % 4] += e
        total = (totals[0] + totals[1]) + (totals[2] + totals[3])
        total = jnp.broadcast_to(jnp.sum(total, axis=0, keepdims=True), (CLS, HALF))
        total = total + xor_lanes(total, 16)
        total = total + xor_lanes(total, 32)
        stats += [top, total]
    out = stats[3]
    line = lax.broadcasted_iota(jnp.int32, (CLS, HALF), 0)
    for r in (2, 1, 0):
        out = jnp.where(line == r, stats[r], out)
    stat_ref[0] = out


def factors(side, got_refs, stat_ref, nblocks, n):
    stats = [
        xor_slots(got_refs[low][high, n ^ high], low) for high in range(nblocks) for low in range(SLOTS)
    ]
    spread = lambda x, r: jnp.broadcast_to(x[r : r + 1], (8, HALF))
    pairs = [(spread(x, r), spread(x, r + 1)) for x in stats for r in (0, 2)]
    best = pairs[0][0]
    for top, _ in pairs[1:]:
        best = jnp.maximum(best, top)
    evidence = jnp.zeros((8, HALF), F32)
    for top, total in pairs:
        evidence = evidence + total * jnp.exp(top - best)
    factor = jnp.where(live_lanes((8, HALF)), jnp.exp(spread(stat_ref[0], 2 * side) - best) / evidence, 0.0)
    return factor, best + jnp.log(evidence)


def spread_kernel(e_ref, far_ref, own_ref):
    turn = lax.broadcasted_iota(jnp.int32, (8, HALF), 1) % 16 // 4
    for side, out_ref in enumerate((own_ref, far_ref)):

        def weights(i):
            i = i % ROT
            w = e_ref[0, side, i * 8 : i * 8 + 8]
            return jnp.where(turn == 0, w, 0.0), jnp.where(turn == 1, w, 0.0)

        def two_turns(now, before):
            return now[0] + pltpu.roll(before[0], 4, 1), pltpu.roll(now[1], HALF - 4, 1) + before[1]

        plain = [weights(i) for i in (-3, -2, -1)]
        pairs = [two_turns(plain[1], plain[0]), two_turns(plain[2], plain[1])]
        before = plain[2]
        for i in range(ROT):
            now = weights(i)
            pairs.append(two_turns(now, before))
            before = now
            last = pairs.pop(0)
            (a, b), (c, d) = pairs[-1], last
            out_ref[0, i * 8 : i * 8 + 8, :HALF] = a + pltpu.roll(c, 8, 1)
            out_ref[0, i * 8 : i * 8 + 8, HALF:] = b + pltpu.roll(d, 8, 1)


def back_kernel(side, nblocks, *refs):
    got_refs = [refs[k] for k in (0, 1, 3, 2)]
    stat_ref, e_ref = refs[SLOTS : SLOTS + 2]
    x_refs = refs[SLOTS + 2 : 2 * SLOTS + 2]
    keep_ref, send_ref, *log_ref = refs[2 * SLOTS + 2 : -2]
    w_ref, acc_ref = refs[-2:]
    n = pl.program_id(0) if nblocks > 1 else 0
    factor, logs = factors(side, got_refs, stat_ref, nblocks, n)
    if log_ref:

        @pl.when(n == 0)
        def _():
            log_ref[0][...] = logs

    turn = lax.broadcasted_iota(jnp.int32, (8, HALF), 1) % 16 // 4
    low = jnp.where(turn == 0, factor, 0.0)
    high = pltpu.roll(jnp.where(turn == 1, factor, 0.0), HALF - 4, 1)
    low, high = (f + pltpu.roll(f, 4, 1) for f in (low, high))
    low, high = (f + pltpu.roll(f, 8, 1) for f in (low, high))
    both = jnp.concatenate([low, high], axis=1)
    both = jnp.concatenate([both, both], axis=0)
    for i in range(0, REF_ROWS, 16):
        pair = (e_ref[0, i : i + 16] * both).astype(BF16)
        w_ref[i : i + 16] = pair
        w_ref[REF_ROWS + i : REF_ROWS + i + 16] = pair

    turned = jnp.concatenate(
        [w_ref[(STEPS - q) * 32 : (STEPS - q) * 32 + REF_ROWS] for q in range(STEPS)], axis=1
    )
    images = jnp.concatenate([images_of(x_refs, q) for q in range(STEPS)], axis=0)
    made = jnp.dot(turned, images, preferred_element_type=F32)
    if nblocks > 1:
        acc_ref[...] = jnp.where(n == 0, made, acc_ref[...] + made)
        made = acc_ref[...]
    first = lax.axis_index("dom") == 0
    keep_ref[...] = jnp.where(first, made[:, :HALF], made[:, HALF:])
    send_ref[...] = jnp.where(first, made[:, HALF:], made[:, :HALF])


def flat_kernel(a_ref, b_ref, c_ref, out_ref, sum_ref, lines_ref, grid_ref):
    sum_ref[:REF_ROWS] = a_ref[...] + b_ref[...] + c_ref[...].astype(F32)
    lane = lax.broadcasted_iota(jnp.int32, (CLS * 8, HALF), 1)
    for c in range(CLS):
        turns = sum_ref[pl.ds(c, HALF, stride=CLS), :]
        lines_ref[c] = turns.T
    for tile in range(GROUP // HALF):
        made = None
        for h in range(16):
            start = ROT * h - tile * HALF
            if start >= HALF or start + ROT <= 0:
                continue
            part = lines_ref[:, h * 8 : h * 8 + 8, :].reshape(CLS * 8, HALF)
            if start % HALF:
                part = pltpu.roll(part, start % HALF, 1)
            made = part if made is None else jnp.where(lane >= start, part, made)
        grid_ref[tile] = made
        for g in range(8):
            start = g * GROUP + tile * HALF
            out_ref[:, start : start + HALF] = grid_ref[tile, pl.ds(g, CLS, stride=8), :]


def swap(x, axis, bits):
    return lax.ppermute(x, axis, [(i, i ^ bits) for i in range(lax.axis_size(axis))])


def gather_slots(block, relay):
    if lax.axis_size("cls") == 2 * SLOTS:
        if relay:
            r2 = swap(block, "cls", 4)
            r1 = swap(block, "cls", 2)
            r3 = swap(r2, "cls", 2)
        else:
            r1, r2, r3 = (swap(block, "cls", bits) for bits in (2, 4, 6))
        return [x[None] for x in (block, r1, r2, r3)]
    slots = block[None]
    bits = 2
    while bits < lax.axis_size("cls"):
        slots = jnp.concatenate([slots, swap(slots, "cls", bits)], axis=0)
        bits *= 2
    return [slots[s::SLOTS] for s in range(SLOTS)]


def call(name, body, nblocks, inputs, outputs, scratch, micros=1, vmem=VMEM):
    def spec(shape, kind):
        if kind == "any":
            return pl.BlockSpec(memory_space=pltpu.HBM)
        if nblocks == 1:
            return pl.BlockSpec(memory_space=pltpu.VMEM)
        rest = (0,) * (len(shape) - 1)
        if kind == "block":
            return pl.BlockSpec((1,) + shape[1:], lambda n: (n,) + rest)
        return pl.BlockSpec(shape, lambda n: (0,) + rest)

    grid = {"grid": (nblocks,)} if nblocks > 1 else {}
    return pl.pallas_call(
        body,
        out_shape=tuple(jax.ShapeDtypeStruct(shape, dtype) for shape, dtype, _ in outputs),
        in_specs=[spec(x.shape, kind) for x, kind in inputs],
        out_specs=tuple(spec(shape, kind) for shape, _, kind in outputs),
        scratch_shapes=scratch,
        compiler_params=pltpu.CompilerParams(vmem_limit_bytes=vmem),
        cost_estimate=pl.CostEstimate(flops=micros * 10**9, bytes_accessed=micros * 10**6, transcendentals=0),
        name=name,
        **grid,
    )(*[x for x, _ in inputs])


def per_device(particles, references, class_lists, offsets, inv_noise):
    holders = lax.axis_size("cls")
    nblocks = holders // 2 // SLOTS
    nbit = -(-holders * CLS // LANES)
    extra = -(-(8 * nbit + 8) // 16) * 16
    rows = ROWS + extra

    def scratch(count):
        return [
            pltpu.VMEM((GROUP // HALF, count * 16, HALF), F32),
            pltpu.VMEM((count, 2, 16, 8, HALF), F32),
            pltpu.VMEM((2, ROT * count, HALF), F32),
        ]

    moves = jnp.transpose(offsets, (1, 2, 0))
    (block,) = call(
        "particle_turns",
        lambda *a: particle_kernel(nbit, *a),
        1,
        [(particles, "any"), (class_lists, "any"), (moves, "any")],
        [((rows, LANES), BF16, "all")],
        [
            pltpu.VMEM(particles.shape, BF16),
            pltpu.VMEM(class_lists.shape, jnp.int32),
            pltpu.SMEM(moves.shape, jnp.int32),
        ]
        + scratch(PER_DEV)
        + [pltpu.SemaphoreType.DMA((3,))],
        vmem=60 * 1024 * 1024,
    )
    slots = gather_slots(block, True)
    far_references = swap(references, "cls", 1)

    weights = jnp.repeat(inv_noise.reshape(8, 8).T, 2, axis=0).reshape(1, HALF)
    weights = jnp.concatenate([weights, weights], axis=1)
    turned = ((2 * REF_ROWS, LANES), BF16, "all")
    freq = ((HALF_TURN, HALF), F32, "all")
    own_refs, fx, fy = call(
        "own_references", reference_kernel, 1, [(references, "all"), (weights, "all")], [turned, freq, freq], scratch(CLS)
    )
    (far_refs,) = call(
        "far_references", reference_kernel, 1, [(far_references, "all"), (weights, "all")], [turned], scratch(CLS)
    )

    bit_rows = 16 * -(-nbit // 2)
    images, bits = [], []
    for slot in slots[:-1]:
        x, b = call(
            "shifted",
            lambda *a: shift_kernel(nbit, *a),
            nblocks,
            [(slot, "block"), (fx, "all"), (fy, "all")],
            [((nblocks, STEPS, CODED, LANES), BF16, "block"), ((nblocks, bit_rows, LANES), BF16, "block")],
            [],
        )
        images.append(x)
        bits.append(b)

    last, expo, stat = call(
        "scores",
        lambda *a: score_kernel(nbit, *a),
        nblocks,
        [(x, "block") for x in images + bits + slots[-1:]] + [(fx, "all"), (fy, "all")] + [(own_refs, "all"), (far_refs, "all")],
        [((nblocks, STEPS, CODED, LANES), BF16, "block"), ((nblocks, 2, REF_ROWS, HALF), F32, "block"), ((nblocks, 8, HALF), F32, "block")],
        [
            pltpu.VMEM((1, bit_rows, LANES), BF16),
            pltpu.VMEM((2, REF_ROWS, LANES), F32),
            pltpu.VMEM((2, REF_ROWS, HALF), F32),
        ],
    )
    images.append(last)
    got = gather_slots(stat, False)

    wide = ((nblocks, REF_ROWS, LANES), F32, "block")
    far_expo, own_expo = call("spread", spread_kernel, nblocks, [(expo, "block")], [wide, wide], [])

    def back(name, side, expo, more):
        half = ((REF_ROWS, HALF), F32, "all")
        return call(
            name,
            lambda *a: back_kernel(side, nblocks, *a),
            nblocks,
            [(g, "all") for g in [got[k] for k in (0, 1, 3, 2)]] + [(stat, "block"), (expo, "block")] + [(x, "block") for x in images],
            [half, half] + more,
            [pltpu.VMEM((2 * REF_ROWS, LANES), BF16), pltpu.VMEM((REF_ROWS, LANES), F32)],
            4,
        )

    far_keep, far_send = back("far_sums", 1, far_expo, [])
    far_got = swap(far_send, "dom", 1)
    keep, send, logs = back("own_sums", 0, own_expo, [((8, HALF), F32, "all")])
    own_got = swap(send, "dom", 1)
    far_sum = swap((far_keep + far_got).astype(BF16), "cls", 1)
    (sums,) = call(
        "flat_rows",
        flat_kernel,
        1,
        [(keep, "all"), (own_got, "all"), (far_sum, "all")],
        [((CLS, GROUP * 8), F32, "all")],
        [
            pltpu.VMEM((HALF * CLS, HALF), F32),
            pltpu.VMEM((CLS, HALF, HALF), F32),
            pltpu.VMEM((GROUP // HALF, CLS * 8, HALF), F32),
        ],
    )
    return sums, logs[0, :PER_DEV]


def solution(mesh):
    placed = (
        P(("groups", "cls", "dom"), None),
        P(("groups", "cls"), None),
        P(("groups", "cls", "dom"), None),
        P(("groups", "cls", "dom"), None, None),
        P(),
    )
    return jax.shard_map(
        per_device,
        mesh=mesh,
        in_specs=placed,
        out_specs=(P(("groups", "cls"), "dom"), P(("groups", "cls", "dom"))),
        check_vma=False,
    )
```
